512 devices in a mesh: seq: 128 (over x_hi, z, y), ch: 4 (over x_lo, core).
Axes of the slice: x: 4 (x_hi: 2, x_lo: 2; x = x_hi * 2 + x_lo), y: 8, z: 8, core: 2. Of those that a mesh axis runs over, the one named last changes fastest.
Arguments:
- tokens: int32 [65536], P('seq'), may hold values from 0 to 3
- hidden: bfloat16 [65536, 1024], P('seq', 'ch'), may hold values from -6 to 6
- embedding: bfloat16 [4, 1024], P(None, 'ch'), may hold values from -6 to 6
- w_in: bfloat16 [1024, 1024], P(None, 'ch'), may hold values from -0.1875 to 0.1875
- w_gate: bfloat16 [1024, 1024], P(None, 'ch'), may hold values from -0.1875 to 0.1875
- conv_w: float32 [3, 4, 1024], P(None, None, 'ch'), may hold values from -3 to 3
- channel_order: int32 [1024], replicated, may hold values from 0 to 1023, each once
- gain: float32 [1024], replicated, may hold values from 0.5 to 1.5
- w_out: bfloat16 [1024, 1024], P(None, 'ch'), may hold values from -0.1875 to 0.1875
- cotangent: bfloat16 [65536, 1024], P('seq', 'ch'), may hold values from -6 to 6
Outputs:
- output: bfloat16 [65536, 1024], P('seq', 'ch')
- grad_in: bfloat16 [1024, 1024], P(None, 'ch')
- grad_gate: bfloat16 [1024, 1024], P(None, 'ch')
- grad_out: bfloat16 [1024, 1024], P(None, 'ch')
- grad_conv: float32 [3, 4, 1024], P(None, None, 'ch')
The draws below stay inside these ranges and needn't reach their ends.
Inputs may be any that keep to these rules, and one draw needn't show every extreme that they name: `channel_order`: each channel index once.
All inputs are finite; a program needn't handle non-finite values.
Results may differ from the reference program's by a relative error of at most 0.025.
Values may be sent and summed in bfloat16 or wider, within the bound.
A program may use at most 64 MiB of HBM per device.

```python
import jax
import jax.numpy as jnp
from jax import lax

D = 1024
LENGTH = 65536
N_CH = 4


def place_ends(result, key, smallest, largest):
    place = [jax.random.randint(jax.random.fold_in(key, axis), (), 0, length) for axis, length in enumerate(result.shape)]
    widest = result.shape.index(max(result.shape))
    neighbour = place[:widest] + [(place[widest] + 1) % result.shape[widest]] + place[widest + 1:]
    return result.at[tuple(place)].set(smallest).at[tuple(neighbour)].set(largest)


def shard_levels(own_key, extent, split, smallest, top_value):
    level, own = 1.0, jax.random.fold_in(own_key, 6)
    for dim, blocks in split:
        draws = jnp.exp(jax.random.uniform(jax.random.fold_in(own, dim), (blocks,), jnp.float32, smallest / len(split), top_value / len(split)))
        level = level * jnp.repeat(draws, extent[dim] // blocks).reshape([-1 if axis == dim else 1 for axis in range(len(extent))])
    return level


def centred(stream_key, dims, deviation, limit, shards=(), held_as=jnp.bfloat16):
    entries = deviation * jax.random.normal(stream_key, dims, jnp.float32)
    if shards:
        entries = entries * shard_levels(stream_key, dims, shards, -0.22, 0.18)
    return jnp.clip(entries, -limit, limit).astype(held_as)


def setup_inputs(seed: int = 0) -> dict:
    arg_keys = jax.random.split(jax.random.key(seed), 11)
    tokens = place_ends(jax.random.randint(arg_keys[0], (LENGTH,), 0, 4), jax.random.fold_in(arg_keys[0], 1), 0, 3).astype(jnp.int32)
    hidden = centred(arg_keys[1], (LENGTH, D), 1.0, 6.0, ((0, 128), (1, 4)))
    embedding = centred(arg_keys[2], (4, D), 1.0, 6.0, ((1, 4),))
    w_in = centred(arg_keys[3], (D, D), D ** -0.5, 0.1875, ((1, 4),))
    w_gate = centred(arg_keys[4], (D, D), D ** -0.5, 0.1875, ((1, 4),))
    conv_w = centred(arg_keys[5], (3, 4, D), 0.5, 3.0, ((2, 4),), jnp.float32)
    channel_order = jax.random.permutation(arg_keys[6], D).astype(jnp.int32)
    gain = jnp.clip(1.0 + 0.1 * jax.random.normal(arg_keys[7], (D,), jnp.float32), 0.5, 1.5)
    w_out = centred(arg_keys[8], (D, D), D ** -0.5, 0.1875, ((1, 4),))
    cotangent = centred(arg_keys[9], (LENGTH, D), 1.0, 6.0, ((0, 128), (1, 4)))
    return {"tokens": tokens, "hidden": hidden, "embedding": embedding, "w_in": w_in, "w_gate": w_gate, "conv_w": conv_w, "channel_order": channel_order, "gain": gain, "w_out": w_out, "cotangent": cotangent}


DILATIONS = (1, 8, 64)
EPSILON = 1e-06

def conv_forward(source, weights, dilation):
    length = source.shape[0]
    padded = jnp.pad(source, ((2 * dilation, 2 * dilation), (0, 0)))
    total = jnp.zeros(source.shape, jnp.float32)
    for position in range(4):
        begin = 2 * dilation + (position - 2) * dilation
        total = total + weights[position][None, :] * padded[begin:begin + length].astype(jnp.float32)
    return (total, padded)

def conv_backward(upstream, weights, padded_source, dilation):
    length = upstream.shape[0]
    padded_grad = jnp.pad(upstream, ((2 * dilation, 2 * dilation), (0, 0)))
    upstream_wide = upstream.astype(jnp.float32)
    total = jnp.zeros(upstream.shape, jnp.float32)
    weight_rows = []
    for position in range(4):
        begin = 2 * dilation - (position - 2) * dilation
        total = total + weights[position][None, :] * padded_grad[begin:begin + length].astype(jnp.float32)
        start = 2 * dilation + (position - 2) * dilation
        weight_rows.append(lax.optimization_barrier(jnp.sum(upstream_wide * padded_source[start:start + length].astype(jnp.float32), axis=0)))
    return (total, jnp.stack(weight_rows))

def reference(tokens, hidden, embedding, w_in, w_gate, conv_w, channel_order, gain, w_out, cotangent):
    width_full = hidden.shape[1]
    width_group = width_full // N_CH
    block_in = (hidden.astype(jnp.float32) + embedding[tokens].astype(jnp.float32)).astype(jnp.bfloat16)
    projected = jnp.dot(block_in, w_in, preferred_element_type=jnp.float32).astype(jnp.bfloat16)
    gate_pre = jnp.dot(block_in, w_gate, preferred_element_type=jnp.float32)
    saved = []
    current = projected
    for level in range(3):
        total, padded = conv_forward(current, conv_w[level], DILATIONS[level])
        saved.append(padded)
        current = total.astype(jnp.bfloat16)
    gate_act = jax.nn.silu(gate_pre)
    gated = (current.astype(jnp.float32) * gate_act).astype(jnp.bfloat16)
    combined = gated.astype(jnp.float32) + gated[::-1][:, channel_order].astype(jnp.float32)
    inv_scale = lax.rsqrt(lax.optimization_barrier(jnp.mean(combined * combined, axis=1, keepdims=True)) + EPSILON)
    normalized = (combined * inv_scale * gain[None, :]).astype(jnp.bfloat16)
    output = (block_in.astype(jnp.float32) + jnp.dot(normalized, w_out, preferred_element_type=jnp.float32)).astype(jnp.bfloat16)
    grad_norm = jnp.zeros(combined.shape, jnp.float32)
    for group in range(N_CH):
        low = group * width_group
        part = jnp.dot(cotangent[:, low:low + width_group], w_out[:, low:low + width_group].T, preferred_element_type=jnp.float32)
        grad_norm = grad_norm + part.astype(jnp.bfloat16).astype(jnp.float32)
    hat = combined * inv_scale
    scaled = grad_norm * gain[None, :]
    row_total = lax.optimization_barrier(jnp.sum(scaled * hat, axis=1, keepdims=True))
    grad_comb = (inv_scale * (scaled - hat * row_total / width_full)).astype(jnp.bfloat16)
    inverse = jnp.zeros_like(channel_order).at[channel_order].set(jnp.arange(width_full, dtype=jnp.int32))
    grad_gated = grad_comb.astype(jnp.float32) + grad_comb[:, inverse][::-1].astype(jnp.float32)
    grad_level = (grad_gated * gate_act).astype(jnp.bfloat16)
    sigmoid_gate = jax.nn.sigmoid(gate_pre)
    grad_gate_pre = (grad_gated * current.astype(jnp.float32) * sigmoid_gate * (1.0 + gate_pre * (1.0 - sigmoid_gate))).astype(jnp.bfloat16)
    tap_grads = [None, None, None]
    for level in (2, 1, 0):
        total, tap_grads[level] = conv_backward(grad_level, conv_w[level], saved[level], DILATIONS[level])
        grad_level = total.astype(jnp.bfloat16)
    contract_rows = (((0,), (0,)), ((), ()))
    grad_in = lax.dot_general(block_in, grad_level, contract_rows, preferred_element_type=jnp.float32)
    grad_gate = lax.dot_general(block_in, grad_gate_pre, contract_rows, preferred_element_type=jnp.float32)
    grad_out = lax.dot_general(normalized, cotangent, contract_rows, preferred_element_type=jnp.float32)
    return (output, grad_in.astype(jnp.bfloat16), grad_gate.astype(jnp.bfloat16), grad_out.astype(jnp.bfloat16), jnp.stack(tap_grads))
```

```python
import functools

import jax
import jax.numpy as jnp
from jax import lax
from jax.experimental import pallas as pl
from jax.experimental.pallas import tpu as pltpu
from jax.sharding import PartitionSpec as P

DILATIONS = (1, 8, 64)
EPSILON = 1e-06


def extended(cells, sides, width):
    for axis, dim in sides:
        count = lax.axis_size(axis)
        ends = count - 1
        head = lax.slice_in_dim(cells, 0, width, axis=dim)
        tail = lax.slice_in_dim(cells, cells.shape[dim] - width, cells.shape[dim], axis=dim)
        cells = jnp.concatenate(
            [
                lax.ppermute(tail, axis, [(i, (i + 1) % count) for i in range(ends)]),
                cells,
                lax.ppermute(head, axis, [((i + 1) % count, i) for i in range(ends)]),
            ],
            axis=dim,
        )
    return cells


def mirror_blocks(block, axis):
    count = lax.axis_size(axis)
    return lax.ppermute(block, axis, [(i, count - 1 - i) for i in range(count)])


def conv_apply(padded, weights, dilation, rows):
    total = jnp.zeros((rows, padded.shape[1]), jnp.float32)
    for position in range(4):
        begin = 2 * dilation + (position - 2) * dilation
        total = total + weights[position][None, :] * padded[begin : begin + rows].astype(
            jnp.float32
        )
    return total


def conv_transpose(padded_grad, weights, dilation, rows):
    total = jnp.zeros((rows, padded_grad.shape[1]), jnp.float32)
    for position in range(4):
        begin = 2 * dilation - (position - 2) * dilation
        total = total + weights[position][None, :] * padded_grad[begin : begin + rows].astype(
            jnp.float32
        )
    return total


def conv_weight_grad(upstream, padded_source, dilation, rows):
    upstream_wide = upstream.astype(jnp.float32)
    weight_rows = []
    for position in range(4):
        start = 2 * dilation + (position - 2) * dilation
        weight_rows.append(
            jnp.sum(upstream_wide * padded_source[start : start + rows].astype(jnp.float32), axis=0)
        )
    return jnp.stack(weight_rows)

MESH = pl.DeviceIdType.MESH


def ring_sizes(count):
    return {128: (2, 8, 8), 8: (2, 2, 2), 4: (1, 2, 2)}[count]


def reduce_kernel(
    sizes,
    g0_ref, g1_ref, g2_ref, conv_ref,
    o0_ref, o1_ref, o2_ref, oconv_ref,
    send1, recv1, send2, recv2, whole,
    s1, r1, s2, r2, s3, r3, s4, r4,
):
    xs, zs, ys = sizes
    seq = lax.axis_index("seq")
    my_y = lax.rem(seq, ys)
    my_z = lax.rem(lax.div(seq, ys), zs)
    my_x = lax.div(seq, ys * zs)

    def at(x, z, y):
        return {"seq": (x * zs + z) * ys + y}

    first = (ys, zs)
    second = (zs, ys)
    me1 = (my_y, my_z)
    me2 = (my_z, my_y)

    def first_peer(h, t):
        return at(my_x, my_z, t) if h == 0 else at(my_x, t, my_y)

    def second_peer(h, x, t):
        return at(x, t, my_y) if h == 0 else at(x, my_z, t)

    barrier = pltpu.get_barrier_semaphore()
    greeted = 0
    for h in range(2):
        for d in range(1, first[h]):
            pl.semaphore_signal(
                barrier, inc=1, device_id=first_peer(h, lax.rem(me1[h] + d, first[h])), device_id_type=MESH
            )
            greeted += 1
    for dx in range(1, xs):
        x = lax.rem(my_x + dx, xs)
        for dz in range(zs):
            pl.semaphore_signal(barrier, inc=1, device_id=at(x, lax.rem(my_z + dz, zs), my_y), device_id_type=MESH)
            greeted += 1
        for dy in range(1, ys):
            pl.semaphore_signal(barrier, inc=1, device_id=at(x, my_z, lax.rem(my_y + dy, ys)), device_id_type=MESH)
            greeted += 1

    grads = (g0_ref, g1_ref, g2_ref)
    n = len(grads)
    rows = g0_ref.shape[0]
    conv_rows = conv_ref.shape[0]
    for h in range(2):
        lanes = slice(128 * h, 128 * h + 128)
        size = rows // first[h]
        for k in range(first[h]):
            for g in range(n):
                send1[h, k, g * size : (g + 1) * size, :] = grads[g][k * size : (k + 1) * size, lanes].astype(
                    jnp.bfloat16
                )
            send1[h, k, n * size : n * size + conv_rows, :] = conv_ref[:, lanes].astype(jnp.bfloat16)
    pl.semaphore_wait(barrier, greeted)

    pending = []

    def exchange1(h, slot_src, t, slot_dst):
        return pltpu.make_async_remote_copy(
            src_ref=send1.at[h, slot_src],
            dst_ref=recv1.at[h, slot_dst],
            send_sem=s1.at[h, slot_src],
            recv_sem=r1.at[h, slot_dst],
            device_id=first_peer(h, t),
            device_id_type=MESH,
        )

    for d in range(1, max(first)):
        for h in range(2):
            t = lax.rem(me1[h] + d, first[h])
            copy = exchange1(h, t, t, me1[h])
            copy.start()
            pending.append(copy)

    def exchange2(h, x, t, src, dst):
        return pltpu.make_async_remote_copy(
            src_ref=send2.at[h, src],
            dst_ref=recv2.at[h, dst],
            send_sem=s2.at[h, lax.rem(my_x + x, xs) * second[h] + lax.rem(me2[h] + t, second[h])],
            recv_sem=r2.at[h, dst],
            device_id=second_peer(h, lax.rem(my_x + x, xs), lax.rem(me2[h] + t, second[h])),
            device_id_type=MESH,
        )

    for h in range(2):
        size = rows // first[h]
        part = size // second[h]
        total = send1[h, me1[h]].astype(jnp.float32)
        for d in range(1, first[h]):
            k = lax.rem(me1[h] + d, first[h])
            exchange1(h, k, k, k).wait_recv()
            recv = recv1[h, k].astype(jnp.float32)
            total = total + recv
        recv1[h, me1[h], n * size :, :] = send1[h, me1[h], n * size :, :]
        tail = jnp.zeros((conv_rows, 128), jnp.float32)
        for k in range(first[h]):
            tail = tail + recv1[h, k, n * size :, :].astype(jnp.float32)
        total = total.astype(jnp.bfloat16)
        for k in range(second[h]):
            for g in range(n):
                send2[h, k, g * part : (g + 1) * part, :] = total[g * size + k * part : g * size + (k + 1) * part]
            send2[h, k, n * part :, :] = tail.astype(jnp.bfloat16)
        mine = my_x * second[h] + me2[h]
        for x in range(xs):
            for t in range(second[h]):
                if x or t:
                    copy = exchange2(h, x, t, lax.rem(me2[h] + t, second[h]), mine)
                    copy.start()
                    pending.append(copy)
        recv2[h, mine] = send2[h, me2[h]]

    def exchange3(h, t, slot):
        place = whole.at[h, me1[h], slot]
        return pltpu.make_async_remote_copy(
            src_ref=place,
            dst_ref=place,
            send_sem=s3.at[h, t],
            recv_sem=r3.at[h, slot],
            device_id=second_peer(h, my_x, t),
            device_id_type=MESH,
        )

    for h in range(2):
        size = rows // first[h]
        part = size // second[h]
        for x in range(xs):
            for t in range(second[h]):
                if x or t:
                    k = lax.rem(my_x + x, xs) * second[h] + lax.rem(me2[h] + t, second[h])
                    exchange2(h, 0, 1, me2[h], k).wait_recv()
        total = jnp.zeros((n * part + conv_rows, 128), jnp.float32)
        for k in range(xs * second[h]):
            total = total + recv2[h, k].astype(jnp.float32)
        whole[h, me1[h], me2[h]] = total[: n * part].astype(jnp.bfloat16)
        oconv_ref[:, 128 * h : 128 * h + 128] = total[n * part :]
        for d in range(1, second[h]):
            t = lax.rem(me2[h] + d, second[h])
            copy = exchange3(h, t, me2[h])
            copy.start()
            pending.append(copy)

    def exchange4(h, t, slot):
        return pltpu.make_async_remote_copy(
            src_ref=whole.at[h, slot],
            dst_ref=whole.at[h, slot],
            send_sem=s4.at[h, t],
            recv_sem=r4.at[h, slot],
            device_id=first_peer(h, t),
            device_id_type=MESH,
        )

    outs = (o0_ref, o1_ref, o2_ref)

    def place(h, k):
        part = rows // first[h] // second[h]
        size = rows // first[h]
        for m in range(second[h]):
            block = whole[h, k, m]
            for g in range(n):
                at_row = pl.multiple_of(k * size + m * part, part)
                outs[g][pl.ds(at_row, part), 128 * h : 128 * h + 128] = block[g * part : (g + 1) * part]

    for h in range(2):
        for d in range(1, second[h]):
            k = lax.rem(me2[h] + d, second[h])
            exchange3(h, k, k).wait_recv()
        for d in range(1, first[h]):
            t = lax.rem(me1[h] + d, first[h])
            copy = exchange4(h, t, me1[h])
            copy.start()
            pending.append(copy)
    for h in range(2):
        place(h, me1[h])
    for d in range(1, max(first)):
        for h in range(2):
            k = lax.rem(me1[h] + d, first[h])
            exchange4(h, k, k).wait_recv()
            place(h, k)
    for copy in pending:
        copy.wait_send()


def reduce_gradients(g0, g1, g2, conv):
    sizes = ring_sizes(lax.axis_size("seq"))
    xs, zs, ys = sizes
    rows = g0.shape[0]
    conv = jnp.pad(conv, ((0, 4), (0, 0)))
    assert ys == zs
    n = 3
    chunk = n * rows // ys + 16
    part = n * rows // ys // zs
    grad = jax.ShapeDtypeStruct((rows, 256), jnp.bfloat16)
    vmem = pl.BlockSpec(memory_space=pltpu.VMEM)
    dma = pltpu.SemaphoreType.DMA
    return pl.pallas_call(
        functools.partial(reduce_kernel, sizes),
        out_shape=(grad, grad, grad, jax.ShapeDtypeStruct(conv.shape, jnp.float32)),
        in_specs=[vmem] * 4,
        out_specs=(vmem,) * 4,
        scratch_shapes=[
            pltpu.VMEM((2, ys, chunk, 128), jnp.bfloat16),
            pltpu.VMEM((2, ys, chunk, 128), jnp.bfloat16),
            pltpu.VMEM((2, zs, part + 16, 128), jnp.bfloat16),
            pltpu.VMEM((2, xs * zs, part + 16, 128), jnp.bfloat16),
            pltpu.VMEM((2, ys, zs, part, 128), jnp.bfloat16),
            dma((2, ys)), dma((2, ys)),
            dma((2, xs * zs)), dma((2, xs * zs)),
            dma((2, zs)), dma((2, zs)),
            dma((2, ys)), dma((2, ys)),
        ],
        compiler_params=pltpu.CompilerParams(
            collective_id=0, has_side_effects=True, vmem_limit_bytes=40 * 1024 * 1024
        ),
    )(g0, g1, g2, conv)


def local(tokens, hidden, embedding, w_in, w_gate, conv_w, channel_order, gain, w_out, cotangent):
    rows = hidden.shape[0]
    width_local = hidden.shape[1]
    width_full = gain.shape[0]
    start_col = lax.axis_index("ch") * width_local
    one_hot = (tokens[:, None] == jnp.arange(4, dtype=jnp.int32)[None, :]).astype(jnp.bfloat16)
    embed_rows = jnp.dot(one_hot, embedding, preferred_element_type=jnp.float32)
    local_input = (hidden.astype(jnp.float32) + embed_rows).astype(jnp.bfloat16)
    full_input = lax.all_gather(local_input, "ch", axis=1, tiled=True)
    projected = jnp.dot(full_input, w_in, preferred_element_type=jnp.float32).astype(jnp.bfloat16)
    gate_pre = jnp.dot(full_input, w_gate, preferred_element_type=jnp.float32)
    saved = []
    current = projected
    for level in range(3):
        dilation = DILATIONS[level]
        padded = extended(current, (("seq", 0),), 2 * dilation)
        saved.append(padded)
        current = conv_apply(padded, conv_w[level], dilation, rows).astype(jnp.bfloat16)
    gate_act = jax.nn.silu(gate_pre)
    gated = (current.astype(jnp.float32) * gate_act).astype(jnp.bfloat16)
    gated_full = lax.all_gather(gated, "ch", axis=1, tiled=True)
    mirrored = lax.all_gather(mirror_blocks(gated, "seq"), "ch", axis=1, tiled=True)
    mirror_full = mirrored[::-1]
    combined = gated_full.astype(jnp.float32) + jnp.take(mirror_full, channel_order, axis=1).astype(
        jnp.float32
    )
    inv_scale = lax.rsqrt(jnp.mean(combined * combined, axis=1, keepdims=True) + EPSILON)
    normalized = (combined * inv_scale * gain[None, :]).astype(jnp.bfloat16)
    output = (
        local_input.astype(jnp.float32)
        + jnp.dot(normalized, w_out, preferred_element_type=jnp.float32)
    ).astype(jnp.bfloat16)
    grad_terms = lax.dot_general(
        cotangent, w_out, (((1,), (1,)), ((), ())), preferred_element_type=jnp.float32
    )
    grad_norm = lax.psum_scatter(
        grad_terms.astype(jnp.bfloat16), "ch", scatter_dimension=1, tiled=True
    ).astype(jnp.float32)
    own_hat = lax.dynamic_slice_in_dim(combined, start_col, width_local, 1) * inv_scale
    own_gain = lax.dynamic_slice_in_dim(gain, start_col, width_local, 0)
    scaled = grad_norm * own_gain[None, :]
    row_total = lax.psum(jnp.sum(scaled * own_hat, axis=1, keepdims=True), "ch")
    grad_comb = (inv_scale * (scaled - own_hat * row_total / width_full)).astype(jnp.bfloat16)
    grad_full = lax.all_gather(grad_comb, "ch", axis=1, tiled=True)
    inverse = (
        jnp.zeros_like(channel_order).at[channel_order].set(jnp.arange(width_full, dtype=jnp.int32))
    )
    own_inverse = lax.dynamic_slice_in_dim(inverse, start_col, width_local, 0)
    grad_mirror = jnp.take(grad_full, own_inverse, axis=1)
    grad_mirror = mirror_blocks(grad_mirror, "seq")
    grad_gated = grad_comb.astype(jnp.float32) + grad_mirror[::-1].astype(jnp.float32)
    upstream = (grad_gated * gate_act).astype(jnp.bfloat16)
    sigmoid_gate = jax.nn.sigmoid(gate_pre)
    grad_gate_pre = (
        grad_gated
        * current.astype(jnp.float32)
        * sigmoid_gate
        * (1.0 + gate_pre * (1.0 - sigmoid_gate))
    ).astype(jnp.bfloat16)
    tap_grads = [None, None, None]
    for level in (2, 1, 0):
        dilation = DILATIONS[level]
        padded_grad = extended(upstream, (("seq", 0),), 2 * dilation)
        tap_grads[level] = conv_weight_grad(upstream, saved[level], dilation, rows)
        upstream = conv_transpose(padded_grad, conv_w[level], dilation, rows).astype(jnp.bfloat16)
    contract_rows = (((0,), (0,)), ((), ()))
    local_in = lax.dot_general(
        full_input, upstream, contract_rows, preferred_element_type=jnp.float32
    )
    local_gate = lax.dot_general(
        full_input, grad_gate_pre, contract_rows, preferred_element_type=jnp.float32
    )
    local_out = lax.dot_general(
        normalized, cotangent, contract_rows, preferred_element_type=jnp.float32
    )
    sum_in, sum_gate, sum_out, sum_conv = reduce_gradients(
        local_in, local_gate, local_out, jnp.concatenate(tap_grads)
    )
    return output, sum_in, sum_gate, sum_out, sum_conv[:12].reshape(3, 4, width_local)


def solution(mesh):
    placed = (
        P("seq"),
        P("seq", "ch"),
        P(None, "ch"),
        P(None, "ch"),
        P(None, "ch"),
        P(None, None, "ch"),
        P(),
        P(),
        P(None, "ch"),
        P("seq", "ch"),
    )
    return jax.shard_map(
        local,
        mesh=mesh,
        in_specs=placed,
        out_specs=(
            P("seq", "ch"),
            P(None, "ch"),
            P(None, "ch"),
            P(None, "ch"),
            P(None, None, "ch"),
        ),
        check_vma=False,
    )
```

```python
import functools

import jax
import jax.numpy as jnp
from jax import lax
from jax.experimental import pallas as pl
from jax.experimental.pallas import tpu as pltpu
from jax.sharding import PartitionSpec as P

DILATIONS = (1, 8, 64)
EPSILON = 1e-06
MESH = pl.DeviceIdType.MESH
BF16 = jnp.bfloat16
F32 = jnp.float32

FWD_LEFT, FWD_RIGHT = 160, 80
BWD_LEFT, BWD_RIGHT = 80, 160
CHUNK = 64
SENDS = 160
RECEIVES = 192


def ring_sizes(count):
    return {128: (2, 8, 8), 8: (2, 2, 2), 4: (1, 2, 2)}[count]


def dot(a, b, contract):
    return lax.dot_general(a, b, ((contract[:1], contract[1:]), ((), ())), preferred_element_type=F32)


def pieces(lo, hi):
    return [(start, min(CHUNK, hi - start)) for start in range(lo, hi, CHUNK)]


def block_kernel(
    sizes, groups,
    tokens_ref, hidden_ref, embedding_ref, w_in_ref, w_gate_ref, conv_w_ref, order_ref, gain_ref, w_out_ref, cot_ref,
    output_ref, grad_in_ref, grad_gate_ref, grad_out_ref, grad_conv_ref,
    block_in, embed, level0, level1, level2, level3, gate_pre, halo_send, halo_recv, halo_late,
    gated, both, permute, cot_mix, term_send, term_recv, term_cross, norm_mix, grad_split,
    grad_gated, up3, up2, up1, product_send, product_recv, up3_low, up0_low, gate_low,
    send1, recv1, send2, recv2, whole, send_sem, recv_sem,
):
    xs, zs, ys = sizes
    count = xs * zs * ys
    rows, width = hidden_ref.shape
    full = width * groups
    eighth = rows // (2 * groups)
    half = rows // 2

    seq = lax.axis_index("seq")
    ch = lax.axis_index("ch")
    core = lax.rem(ch, 2)
    x_lo = lax.div(ch, 2)
    sibling = x_lo * 2 + 1 - core
    across = (1 - x_lo) * 2 + core
    diagonal = (1 - x_lo) * 2 + 1 - core
    mirror = count - 1 - seq
    after = lax.rem(seq + 1, count)
    before = lax.rem(seq + count - 1, count)
    my_y = lax.rem(seq, ys)
    my_z = lax.rem(lax.div(seq, ys), zs)
    my_x = lax.div(seq, ys * zs)
    left_live = (seq > 0).astype(F32)
    right_live = (seq < count - 1).astype(F32)

    def at(x, z, y):
        return {"seq": (x * zs + z) * ys + y}

    first = (ys, zs)
    second = (zs, ys)
    me1 = (my_y, my_z)
    me2 = (my_z, my_y)

    def first_peer(h, t):
        return at(my_x, my_z, t) if h == 0 else at(my_x, t, my_y)

    def second_peer(h, x, t):
        return at(x, t, my_y) if h == 0 else at(x, my_z, t)

    def top(q):
        return pl.ds(pl.multiple_of(q * eighth, eighth), eighth)

    def bottom(q):
        return pl.ds(pl.multiple_of(rows - eighth - q * eighth, eighth), eighth)

    barrier = pltpu.get_barrier_semaphore()
    greeted = []

    def greet(device):
        pl.semaphore_signal(barrier, inc=1, device_id=device, device_id_type=MESH)
        greeted.append(0)

    greet({"ch": sibling})
    greet({"ch": across})
    greet({"ch": diagonal})
    for q in range(groups):
        greet({"seq": mirror, "ch": q})
    greet({"seq": after})
    greet({"seq": before})
    for h in range(2):
        for d in range(1, first[h]):
            greet(first_peer(h, lax.rem(me1[h] + d, first[h])))
    for dx in range(1, xs):
        x = lax.rem(my_x + dx, xs)
        for dz in range(zs):
            greet(at(x, lax.rem(my_z + dz, zs), my_y))
        for dy in range(1, ys):
            greet(at(x, my_z, lax.rem(my_y + dy, ys)))

    pending = []
    bases = {}

    def base(name, size):
        if name not in bases:
            bases[name] = sum(taken for _, taken in bases.values()), size
        return bases[name][0]

    def send(src, dst, receive, device):
        copy = pltpu.make_async_remote_copy(
            src_ref=src, dst_ref=dst, send_sem=send_sem.at[len(pending)], recv_sem=recv_sem.at[receive],
            device_id=device, device_id_type=MESH,
        )
        copy.start()
        pending.append(copy)

    def arrived(dst, receive):
        pltpu.make_async_remote_copy(
            src_ref=dst, dst_ref=dst, send_sem=send_sem.at[0], recv_sem=recv_sem.at[receive],
            device_id={"ch": sibling}, device_id_type=MESH,
        ).wait_recv()

    embed[...] = jnp.zeros_like(embed)
    embed[0:4, :] = embedding_ref[...]
    hot = (lax.broadcasted_iota(jnp.int32, (16, rows), 0) == tokens_ref[...]).astype(F32).astype(BF16)
    looked_up = dot(hot, embed[...], (0, 0))
    block_in[ch] = (hidden_ref[...].astype(F32) + looked_up).astype(BF16)
    cot_mix[0:half, :] = cot_ref[0:half, :]

    pl.semaphore_wait(barrier, len(greeted))

    parts = ((rows - FWD_LEFT, FWD_LEFT), (0, FWD_RIGHT), (FWD_RIGHT, rows - FWD_LEFT - FWD_RIGHT))
    gather = base("gather", 3 * groups)

    def gather_part(i, slot):
        return block_in.at[slot, pl.ds(parts[i][0], parts[i][1])]

    def gather_send(i, slot, target):
        send(gather_part(i, slot), gather_part(i, slot), gather + i * groups + slot, {"ch": target})

    def gather_wait(i, slot):
        arrived(gather_part(i, slot), gather + i * groups + slot)

    for i in range(3):
        gather_send(i, ch, across)
        gather_send(i, ch, sibling)
    cot_sem = base("cot", 1)
    send(cot_ref.at[pl.ds(half, half)], cot_mix.at[pl.ds(half, half)], cot_sem, {"seq": mirror})

    for start in range(0, full, 128):
        place = lax.broadcasted_iota(jnp.int32, (128, full), 0) + start
        permute[start : start + 128, :] = (place == order_ref[...]).astype(F32).astype(BF16)
    flip = (
        lax.broadcasted_iota(jnp.int32, (2 * eighth, 2 * eighth), 0)
        + lax.broadcasted_iota(jnp.int32, (2 * eighth, 2 * eighth), 1)
        == 2 * eighth - 1
    ).astype(F32).astype(BF16)

    def project(i, weights):
        start, size = parts[i]
        total = jnp.zeros((size, width), F32)
        for k in range(groups):
            total = total + dot(block_in[k, start : start + size, :], weights[k * width : (k + 1) * width, :], (1, 0))
        return total

    halo = base("halo", 2)
    for i in range(2):
        gather_wait(i, across)
        gather_send(i, across, sibling)
    for i in range(2):
        start, size = parts[i]
        gather_wait(i, sibling)
        gather_wait(i, diagonal)
        projected = project(i, w_in_ref).astype(BF16)
        level0[FWD_LEFT + start : FWD_LEFT + start + size, :] = projected.astype(F32)
        keep = pl.ds(0, FWD_LEFT) if i == 0 else pl.ds(FWD_LEFT, FWD_RIGHT)
        halo_send[keep, :] = projected
        send(halo_send.at[keep], halo_recv.at[keep], halo + i, {"seq": after if i == 0 else before})
    gather_wait(2, across)
    gather_send(2, across, sibling)
    for i in range(2):
        start, size = parts[i]
        gate_pre[start : start + size, :] = project(i, w_gate_ref)

    arrived(cot_mix.at[pl.ds(half, half)], cot_sem)
    for q in range(groups):
        low = rows - eighth - q * eighth
        for part, start in enumerate((q * eighth, low)):
            term_send[q, part * eighth : (part + 1) * eighth, :] = dot(
                cot_mix[start : start + eighth, :], w_out_ref[...], (1, 1)
            ).astype(BF16)
    term = base("term", 3)
    gather_wait(2, sibling)
    gather_wait(2, diagonal)
    for i in range(2):
        target = i * 2 + 1 - core
        send(term_send.at[target], term_recv.at[i], term + i, {"ch": sibling})
    start, size = parts[2]
    level0[FWD_LEFT + start : FWD_LEFT + start + size, :] = project(2, w_in_ref).astype(BF16).astype(F32)
    gate_pre[start : start + size, :] = project(2, w_gate_ref)

    arrived(halo_recv.at[pl.ds(0, FWD_LEFT)], halo)
    arrived(halo_recv.at[pl.ds(FWD_LEFT, FWD_RIGHT)], halo + 1)
    own = FWD_LEFT + rows
    level0[0:FWD_LEFT, :] = halo_recv[0:FWD_LEFT, :].astype(F32) * left_live
    level0[own : own + FWD_RIGHT, :] = halo_recv[FWD_LEFT : FWD_LEFT + FWD_RIGHT, :].astype(F32) * right_live

    def convolve(source, level, sign, lo, hi, live, store):
        dilation = DILATIONS[level]
        for start, size in pieces(lo, hi):
            total = jnp.zeros((size, width), F32)
            for t in range(4):
                begin = start + sign * (t - 2) * dilation
                total = total + conv_w_ref[level, t : t + 1, :] * source[begin : begin + size, :]
            if live is not None:
                total = total * live
            store(start, size, total.astype(BF16).astype(F32))

    def into(target):
        def store(start, size, value):
            target[start : start + size, :] = value
        return store

    for level, (source, target) in enumerate(((level0, level1), (level1, level2))):
        lo, hi = ((8, own + 72), (24, own + 64))[level]
        convolve(source, level, 1, lo, FWD_LEFT, left_live, into(target))
        convolve(source, level, 1, FWD_LEFT, own, None, into(target))
        convolve(source, level, 1, own, hi, right_live, into(target))

    def store_gated(start, size, value):
        start = start - FWD_LEFT
        level3[start : start + size, :] = value
        gate = gate_pre[start : start + size, :]
        gated[start : start + size, :] = (value * (gate * jax.nn.sigmoid(gate))).astype(BF16)

    convolve(level2, 2, 1, FWD_LEFT, own, None, store_gated)

    mix = base("mix", 2 * groups)
    for q in range(groups):
        send(
            gated.at[pl.ds(rows - eighth - q * eighth, eighth)], both.at[ch, pl.ds(eighth, eighth)],
            mix + groups + ch, {"seq": mirror, "ch": q},
        )
    for d in range(1, groups):
        q = lax.rem(ch + d, groups)
        send(gated.at[top(q)], both.at[ch, pl.ds(0, eighth)], mix + ch, {"ch": q})
    both[ch, 0:eighth, :] = gated[top(ch), :]

    for i in range(2):
        arrived(term_recv.at[i], term + i)
    term_send[across] = (term_send[across].astype(F32) + term_recv[1 - x_lo].astype(F32)).astype(BF16)
    send(term_send.at[across], term_cross, term + 2, {"ch": across})
    arrived(term_cross, term + 2)
    grad_norm = term_send[ch].astype(F32) + term_recv[x_lo].astype(F32) + term_cross[...].astype(F32)
    scaled = grad_norm * gain_ref[...]

    for d in range(1, groups):
        q = lax.rem(ch + d, groups)
        arrived(both.at[q, pl.ds(0, eighth)], mix + q)
    for q in range(groups):
        arrived(both.at[q, pl.ds(eighth, eighth)], mix + groups + q)

    mine = jnp.concatenate([both[q] for q in range(groups)], axis=1)
    other = dot(flip, dot(mine, permute[...], (1, 0)).astype(BF16), (1, 0))
    combined = mine.astype(F32) + other
    inv_scale = lax.rsqrt(jnp.mean(combined * combined, axis=1, keepdims=True) + EPSILON)
    hat = combined * inv_scale
    normalized = (hat * gain_ref[...]).astype(BF16)
    norm_mix[top(ch), :] = normalized[:eighth]
    norm_mix[bottom(ch), :] = normalized[eighth:]
    row_total = jnp.sum(scaled * hat, axis=1, keepdims=True)
    grad_comb = (inv_scale * (scaled - hat * (row_total * (1.0 / full)))).astype(BF16)
    turned = dot(flip, dot(grad_comb, permute[...], (1, 1)).astype(BF16), (1, 0))
    returned = (grad_comb.astype(F32) + turned).astype(BF16)
    for q in range(groups):
        grad_split[q] = returned[:, q * width : (q + 1) * width]
    back = base("back", 2 * groups)
    for q in range(groups):
        send(
            grad_split.at[q, pl.ds(eighth, eighth)], grad_gated.at[bottom(ch)],
            back + groups + ch, {"seq": mirror, "ch": q},
        )
    for d in range(1, groups):
        q = lax.rem(ch + d, groups)
        send(grad_split.at[q, pl.ds(0, eighth)], grad_gated.at[top(ch)], back + ch, {"ch": q})
    grad_gated[top(ch), :] = grad_split[ch, 0:eighth, :]

    norm = base("norm", 2 * groups)

    def norm_send(q, target):
        send(norm_mix.at[top(q)], norm_mix.at[top(q)], norm + q, {"ch": target})
        send(norm_mix.at[bottom(q)], norm_mix.at[bottom(q)], norm + groups + q, {"ch": target})

    def norm_wait(q):
        arrived(norm_mix.at[top(q)], norm + q)
        arrived(norm_mix.at[bottom(q)], norm + groups + q)

    norm_send(ch, across)
    norm_send(ch, sibling)
    norm_wait(across)
    norm_send(across, sibling)
    norm_wait(sibling)
    norm_wait(diagonal)
    product = dot(norm_mix[...], w_out_ref[...], (1, 0))
    output_ref[0:half, :] = (block_in[ch, 0:half, :].astype(F32) + product[:half]).astype(BF16)
    product_send[...] = product[half:].astype(BF16)
    product_sem = base("product", 1)
    send(product_send, product_recv, product_sem, {"seq": mirror})

    conv_rows = 16
    size = full // ys
    part = size // zs
    names = ("out", "gate", "in")

    def exchange1(name, h, k):
        g = names.index(name)
        tall = size + (conv_rows if name == "in" else 0)
        return g, pl.ds(g * size, tall), base("sum" + name, 2 * ys) + h * ys + k

    def spread(name, value):
        for h in range(2):
            for k in range(first[h]):
                g = names.index(name)
                send1[h, k, g * size : (g + 1) * size, :] = value[
                    k * size : (k + 1) * size, 128 * h : 128 * h + 128
                ].astype(BF16)
        for d in range(1, ys):
            for h in range(2):
                t = lax.rem(me1[h] + d, first[h])
                _, span, sem = exchange1(name, h, me1[h])
                send(send1.at[h, t, span], recv1.at[h, me1[h], span], sem, first_peer(h, t))

    spread("out", dot(norm_mix[...], cot_mix[...], (0, 0)))

    for d in range(1, groups):
        q = lax.rem(ch + d, groups)
        arrived(grad_gated.at[top(q)], back + q)
    for q in range(groups):
        arrived(grad_gated.at[bottom(q)], back + groups + q)
    own = BWD_LEFT + rows
    for start, tall in pieces(0, rows):
        gate = gate_pre[start : start + tall, :]
        sigmoid = jax.nn.sigmoid(gate)
        grad = grad_gated[start : start + tall, :].astype(F32)
        upstream = (grad * (gate * sigmoid)).astype(BF16)
        up3_low[start : start + tall, :] = upstream
        up3[BWD_LEFT + start : BWD_LEFT + start + tall, :] = upstream.astype(F32)
        gate_low[start : start + tall, :] = (
            grad * level3[start : start + tall, :] * sigmoid * (1.0 + gate * (1.0 - sigmoid))
        ).astype(BF16)
    halo_back = base("halo_back", 2)
    send(up3_low.at[pl.ds(0, BWD_RIGHT)], halo_late.at[pl.ds(BWD_LEFT, BWD_RIGHT)], halo_back, {"seq": before})
    send(
        up3_low.at[pl.ds(rows - BWD_LEFT, BWD_LEFT)], halo_late.at[pl.ds(0, BWD_LEFT)], halo_back + 1, {"seq": after}
    )

    def against_input(value):
        return jnp.concatenate([dot(block_in[k], value, (0, 0)) for k in range(groups)], axis=0)

    spread("gate", against_input(gate_low[...]))
    arrived(halo_late.at[pl.ds(BWD_LEFT, BWD_RIGHT)], halo_back)
    arrived(halo_late.at[pl.ds(0, BWD_LEFT)], halo_back + 1)
    up3[0:BWD_LEFT, :] = halo_late[0:BWD_LEFT, :].astype(F32) * left_live
    up3[own : own + BWD_RIGHT, :] = halo_late[BWD_LEFT : BWD_LEFT + BWD_RIGHT, :].astype(F32) * right_live

    convolve(up3, 2, -1, 64, BWD_LEFT, left_live, into(up2))
    convolve(up3, 2, -1, BWD_LEFT, own, None, into(up2))
    convolve(up3, 2, -1, own, own + 24, right_live, into(up2))
    convolve(up2, 1, -1, 72, BWD_LEFT, left_live, into(up1))
    convolve(up2, 1, -1, BWD_LEFT, own, None, into(up1))
    convolve(up2, 1, -1, own, own + 8, right_live, into(up1))

    def store_last(start, tall, value):
        up0_low[start - BWD_LEFT : start - BWD_LEFT + tall, :] = value.astype(BF16)

    convolve(up1, 0, -1, BWD_LEFT, own, None, store_last)

    taps = []
    for level, (source, upstream) in enumerate(((level0, up1), (level1, up2), (level2, up3))):
        for t in range(4):
            total = jnp.zeros((8, width), F32)
            for start, tall in pieces(0, rows):
                begin = FWD_LEFT + start + (t - 2) * DILATIONS[level]
                term_product = (
                    upstream[BWD_LEFT + start : BWD_LEFT + start + tall, :] * source[begin : begin + tall, :]
                )
                total = total + jnp.sum(term_product.reshape(tall // 8, 8, width), axis=0)
            taps.append(jnp.sum(total, axis=0, keepdims=True))
    taps = jnp.concatenate(taps + [jnp.zeros((conv_rows - 12, width), F32)], axis=0).astype(BF16)
    for h in range(2):
        for k in range(first[h]):
            send1[h, k, 3 * size : 3 * size + conv_rows, :] = taps[:, 128 * h : 128 * h + 128]
    spread("in", against_input(up0_low[...]))

    arrived(product_recv, product_sem)
    output_ref[half:rows, :] = (
        block_in[ch, half:rows, :].astype(F32) + product_recv[...].astype(F32)
    ).astype(BF16)

    over = base("over", 2 * xs * zs)
    for h in range(2):
        total = send1[h, me1[h]].astype(F32)
        for d in range(1, first[h]):
            k = lax.rem(me1[h] + d, first[h])
            for name in names:
                _, span, sem = exchange1(name, h, k)
                arrived(recv1.at[h, k, span], sem)
            total = total + recv1[h, k].astype(F32)
        recv1[h, me1[h], 3 * size :, :] = send1[h, me1[h], 3 * size :, :]
        tail = jnp.zeros((conv_rows, 128), F32)
        for k in range(first[h]):
            tail = tail + recv1[h, k, 3 * size :, :].astype(F32)
        total = total.astype(BF16)
        for k in range(second[h]):
            for g in range(3):
                send2[h, k, g * part : (g + 1) * part, :] = total[g * size + k * part : g * size + (k + 1) * part]
            send2[h, k, 3 * part :, :] = tail.astype(BF16)
        slot = my_x * second[h] + me2[h]
        for dx in range(xs):
            for dt in range(second[h]):
                if dx or dt:
                    x = lax.rem(my_x + dx, xs)
                    t = lax.rem(me2[h] + dt, second[h])
                    send(send2.at[h, t], recv2.at[h, slot], over + h * xs * zs + slot, second_peer(h, x, t))
        recv2[h, slot] = send2[h, me2[h]]

    gather2 = base("gather2", 2 * zs)
    for h in range(2):
        for dx in range(xs):
            for dt in range(second[h]):
                if dx or dt:
                    k = lax.rem(my_x + dx, xs) * second[h] + lax.rem(me2[h] + dt, second[h])
                    arrived(recv2.at[h, k], over + h * xs * zs + k)
        total = jnp.zeros((3 * part + conv_rows, 128), F32)
        for k in range(xs * second[h]):
            total = total + recv2[h, k].astype(F32)
        whole[h, me1[h], me2[h]] = total[: 3 * part].astype(BF16)
        grad_conv_ref[:, 128 * h : 128 * h + 128] = total[3 * part :]
        for d in range(1, second[h]):
            t = lax.rem(me2[h] + d, second[h])
            here = whole.at[h, me1[h], me2[h]]
            send(here, here, gather2 + h * zs + me2[h], second_peer(h, my_x, t))

    gather1 = base("gather1", 2 * ys)
    outs = (grad_out_ref, grad_gate_ref, grad_in_ref)

    def place_rows(h, k):
        for m in range(second[h]):
            block = whole[h, k, m]
            for g in range(3):
                at_row = pl.multiple_of(k * size + m * part, part)
                outs[g][pl.ds(at_row, part), 128 * h : 128 * h + 128] = block[g * part : (g + 1) * part]

    for h in range(2):
        for d in range(1, second[h]):
            k = lax.rem(me2[h] + d, second[h])
            arrived(whole.at[h, me1[h], k], gather2 + h * zs + k)
        for d in range(1, first[h]):
            t = lax.rem(me1[h] + d, first[h])
            here = whole.at[h, me1[h]]
            send(here, here, gather1 + h * ys + me1[h], first_peer(h, t))
    for h in range(2):
        place_rows(h, me1[h])
    for d in range(1, ys):
        for h in range(2):
            k = lax.rem(me1[h] + d, first[h])
            arrived(whole.at[h, k], gather1 + h * ys + k)
            place_rows(h, k)
    for copy in pending:
        copy.wait_send()


def local(tokens, hidden, embedding, w_in, w_gate, conv_w, channel_order, gain, w_out, cotangent):
    rows, width = hidden.shape
    full = gain.shape[0]
    groups = lax.axis_size("ch")
    sizes = ring_sizes(lax.axis_size("seq"))
    xs, zs, ys = sizes
    size = full // ys
    part = size // zs
    eighth = rows // (2 * groups)
    extended = rows + FWD_LEFT + FWD_RIGHT
    vmem = pl.BlockSpec(memory_space=pltpu.VMEM)
    dma = pltpu.SemaphoreType.DMA

    def held(*shape, dtype=BF16):
        return pltpu.VMEM(shape, dtype)

    weight = jax.ShapeDtypeStruct((full, width), BF16)
    output, grad_in, grad_gate, grad_out, grad_conv = pl.pallas_call(
        functools.partial(block_kernel, sizes, groups),
        out_shape=(
            jax.ShapeDtypeStruct((rows, width), BF16), weight, weight, weight, jax.ShapeDtypeStruct((16, width), F32)
        ),
        in_specs=[vmem] * 10,
        out_specs=(vmem,) * 5,
        scratch_shapes=[
            held(groups, rows, width),
            held(16, width),
            held(extended, width, dtype=F32),
            held(extended, width, dtype=F32),
            held(extended, width, dtype=F32),
            held(rows, width, dtype=F32),
            held(rows, width, dtype=F32),
            held(FWD_LEFT + FWD_RIGHT, width),
            held(FWD_LEFT + FWD_RIGHT, width),
            held(BWD_LEFT + BWD_RIGHT, width),
            held(rows, width),
            held(groups, 2 * eighth, width),
            held(full, full),
            held(rows, width),
            held(groups, 2 * eighth, full),
            held(2, 2 * eighth, full),
            held(2 * eighth, full),
            held(rows, full),
            held(groups, 2 * eighth, width),
            held(rows, width),
            held(extended, width, dtype=F32),
            held(extended, width, dtype=F32),
            held(extended, width, dtype=F32),
            held(rows // 2, width),
            held(rows // 2, width),
            held(rows, width),
            held(rows, width),
            held(rows, width),
            held(2, ys, 3 * size + 16, 128),
            held(2, ys, 3 * size + 16, 128),
            held(2, zs, 3 * part + 16, 128),
            held(2, xs * zs, 3 * part + 16, 128),
            held(2, ys, zs, 3 * part, 128),
            dma((SENDS,)),
            dma((RECEIVES,)),
        ],
        compiler_params=pltpu.CompilerParams(
            collective_id=0, has_side_effects=True, vmem_limit_bytes=56 * 1024 * 1024
        ),
    )(
        tokens.reshape(1, rows), hidden, embedding, w_in, w_gate, conv_w, channel_order.reshape(1, full),
        gain.reshape(1, full), w_out, cotangent,
    )
    return output, grad_in, grad_gate, grad_out, grad_conv[:12].reshape(3, 4, width)


def solution(mesh):
    placed = (
        P("seq"),
        P("seq", "ch"),
        P(None, "ch"),
        P(None, "ch"),
        P(None, "ch"),
        P(None, None, "ch"),
        P(),
        P(),
        P(None, "ch"),
        P("seq", "ch"),
    )
    return jax.shard_map(
        local,
        mesh=mesh,
        in_specs=placed,
        out_specs=(
            P("seq", "ch"),
            P(None, "ch"),
            P(None, "ch"),
            P(None, "ch"),
            P(None, None, "ch"),
        ),
        check_vma=False,
    )
```

```python
import functools

import jax
import jax.numpy as jnp
from jax import lax
from jax.experimental import pallas as pl
from jax.experimental.pallas import tpu as pltpu
from jax.sharding import PartitionSpec as P

DILATIONS = (1, 8, 64)
EPSILON = 1e-06
MESH = pl.DeviceIdType.MESH
BF16 = jnp.bfloat16
F32 = jnp.float32

FWD_LEFT, FWD_RIGHT = 160, 80
BWD_LEFT, BWD_RIGHT = 80, 160
CHUNK = 64
SENDS = 224
RECEIVES = 256


def ring_sizes(count):
    return {128: (2, 8, 8), 8: (2, 2, 2), 4: (1, 2, 2)}[count]


def dot(a, b, contract):
    return lax.dot_general(a, b, ((contract[:1], contract[1:]), ((), ())), preferred_element_type=F32)


def pieces(lo, hi):
    return [(start, min(CHUNK, hi - start)) for start in range(lo, hi, CHUNK)]


def block_kernel(
    sizes, groups,
    tokens_in, hidden_in, embedding_in, w_in_in, w_gate_in, conv_w_in, order_in, gain_in, w_out_in, cot_in,
    output_out, grad_in_out, grad_gate_out, grad_out_out, grad_conv_out,
    tokens_ref, hidden_ref, w_in_ref, w_gate_ref, conv_w_ref, order_ref, gain_ref, w_out_ref,
    output_ref, grad_in_ref, grad_gate_ref, grad_out_ref, grad_conv_ref,
    block_in, embed, level0, level1, level2, level3, gate_pre, halo_send, halo_recv, halo_late,
    gated, both, permute, cot_mix, term_send, term_recv, term_cross, norm_mix, grad_split,
    grad_gated, up3, up2, up1, product_send, product_recv, up3_low, up0_low, gate_low,
    send1, recv1, send2, recv2, whole, conv_x, send_sem, recv_sem, local_sem,
):
    xs, zs, ys = sizes
    count = xs * zs * ys
    rows, width = hidden_ref.shape
    full = width * groups
    eighth = rows // (2 * groups)
    half = rows // 2

    seq = lax.axis_index("seq")
    ch = lax.axis_index("ch")
    core = lax.rem(ch, 2)
    x_lo = lax.div(ch, 2)
    sibling = x_lo * 2 + 1 - core
    across = (1 - x_lo) * 2 + core
    diagonal = (1 - x_lo) * 2 + 1 - core
    mirror = count - 1 - seq
    after = lax.rem(seq + 1, count)
    before = lax.rem(seq + count - 1, count)
    my_y = lax.rem(seq, ys)
    my_z = lax.rem(lax.div(seq, ys), zs)
    my_x = lax.div(seq, ys * zs)
    left_live = (seq > 0).astype(F32)
    right_live = (seq < count - 1).astype(F32)

    def at(x, z, y):
        return {"seq": (x * zs + z) * ys + y}

    first = (ys, zs)
    second = (zs, ys)
    me1 = (my_y, my_z)
    me2 = (my_z, my_y)

    def first_peer(h, t):
        return at(my_x, my_z, t) if h == 0 else at(my_x, t, my_y)

    def second_peer(h, x, t):
        return at(x, t, my_y) if h == 0 else at(x, my_z, t)

    def top(q):
        return pl.ds(pl.multiple_of(q * eighth, eighth), eighth)

    def bottom(q):
        return pl.ds(pl.multiple_of(rows - eighth - q * eighth, eighth), eighth)

    barrier = pltpu.get_barrier_semaphore()
    greeted = []

    def greet(device):
        pl.semaphore_signal(barrier, inc=1, device_id=device, device_id_type=MESH)
        greeted.append(0)

    greet({"ch": sibling})
    greet({"ch": across})
    greet({"ch": diagonal})
    for q in range(groups):
        greet({"seq": mirror, "ch": q})
    greet({"seq": after})
    greet({"seq": before})
    for h in range(2):
        for d in range(1, first[h]):
            greet(first_peer(h, lax.rem(me1[h] + d, first[h])))
    for dx in range(1, xs):
        x = lax.rem(my_x + dx, xs)
        for dz in range(zs):
            greet(at(x, lax.rem(my_z + dz, zs), my_y))
        for dy in range(1, ys):
            greet(at(x, my_z, lax.rem(my_y + dy, ys)))

    pending = []
    bases = {}

    def base(name, size):
        if name not in bases:
            bases[name] = sum(taken for _, taken in bases.values()), size
        return bases[name][0]

    def send(src, dst, receive, device):
        copy = pltpu.make_async_remote_copy(
            src_ref=src, dst_ref=dst, send_sem=send_sem.at[len(pending)], recv_sem=recv_sem.at[receive],
            device_id=device, device_id_type=MESH,
        )
        copy.start()
        pending.append(copy)

    def arrived(dst, receive):
        pltpu.make_async_remote_copy(
            src_ref=dst, dst_ref=dst, send_sem=send_sem.at[0], recv_sem=recv_sem.at[receive],
            device_id={"ch": sibling}, device_id_type=MESH,
        ).wait_recv()

    embed[...] = jnp.zeros_like(embed)
    loads = {}
    for name, src, dst in (
        ("tokens", tokens_in, tokens_ref),
        ("embedding", embedding_in, embed.at[pl.ds(0, 4)]),
        ("hidden", hidden_in, hidden_ref),
        ("cot", cot_in.at[pl.ds(0, half)], cot_mix.at[pl.ds(0, half)]),
        ("order", order_in, order_ref),
        ("w_in", w_in_in, w_in_ref),
        ("w_gate", w_gate_in, w_gate_ref),
        ("w_out", w_out_in, w_out_ref),
        ("conv_w", conv_w_in, conv_w_ref),
        ("gain", gain_in, gain_ref),
    ):
        loads[name] = pltpu.make_async_copy(src, dst, local_sem.at[len(loads)])
        loads[name].start()
    stores = []

    def store_out(src, dst):
        copy = pltpu.make_async_copy(src, dst, local_sem.at[len(loads) + len(stores)])
        copy.start()
        stores.append(copy)

    for name in ("tokens", "embedding", "hidden"):
        loads[name].wait()
    hot = (lax.broadcasted_iota(jnp.int32, (16, rows), 0) == tokens_ref[...]).astype(F32).astype(BF16)
    looked_up = dot(hot, embed[...], (0, 0))
    block_in[ch] = (hidden_ref[...].astype(F32) + looked_up).astype(BF16)

    pl.semaphore_wait(barrier, len(greeted))

    parts = ((rows - FWD_LEFT, FWD_LEFT), (0, FWD_RIGHT), (FWD_RIGHT, rows - FWD_LEFT - FWD_RIGHT))
    gather = base("gather", 3 * groups)

    def gather_part(i, slot):
        return block_in.at[slot, pl.ds(parts[i][0], parts[i][1])]

    def gather_send(i, slot, target):
        send(gather_part(i, slot), gather_part(i, slot), gather + i * groups + slot, {"ch": target})

    def gather_wait(i, slot):
        arrived(gather_part(i, slot), gather + i * groups + slot)

    for i in range(3):
        gather_send(i, ch, across)
        gather_send(i, ch, sibling)
    cot_sem = base("cot", 1)
    send(cot_in.at[pl.ds(half, half)], cot_mix.at[pl.ds(half, half)], cot_sem, {"seq": mirror})

    loads["order"].wait()
    for start in range(0, full, 128):
        place = lax.broadcasted_iota(jnp.int32, (128, full), 0) + start
        permute[start : start + 128, :] = (place == order_ref[...]).astype(F32).astype(BF16)
    flip = (
        lax.broadcasted_iota(jnp.int32, (2 * eighth, 2 * eighth), 0)
        + lax.broadcasted_iota(jnp.int32, (2 * eighth, 2 * eighth), 1)
        == 2 * eighth - 1
    ).astype(F32).astype(BF16)

    def project(i, weights):
        start, size = parts[i]
        total = jnp.zeros((size, width), F32)
        for k in range(groups):
            total = total + dot(block_in[k, start : start + size, :], weights[k * width : (k + 1) * width, :], (1, 0))
        return total

    loads["w_in"].wait()
    halo = base("halo", 2)
    for i in range(2):
        gather_wait(i, across)
        gather_send(i, across, sibling)
    for i in range(2):
        start, size = parts[i]
        gather_wait(i, sibling)
        gather_wait(i, diagonal)
        projected = project(i, w_in_ref).astype(BF16)
        level0[FWD_LEFT + start : FWD_LEFT + start + size, :] = projected.astype(F32)
        keep = pl.ds(0, FWD_LEFT) if i == 0 else pl.ds(FWD_LEFT, FWD_RIGHT)
        halo_send[keep, :] = projected
        send(halo_send.at[keep], halo_recv.at[keep], halo + i, {"seq": after if i == 0 else before})
    gather_wait(2, across)
    gather_send(2, across, sibling)
    loads["w_gate"].wait()
    for i in range(2):
        start, size = parts[i]
        gate_pre[start : start + size, :] = project(i, w_gate_ref)

    loads["w_out"].wait()
    loads["cot"].wait()
    arrived(cot_mix.at[pl.ds(half, half)], cot_sem)
    for q in range(groups):
        low = rows - eighth - q * eighth
        for part, start in enumerate((q * eighth, low)):
            term_send[q, part * eighth : (part + 1) * eighth, :] = dot(
                cot_mix[start : start + eighth, :], w_out_ref[...], (1, 1)
            ).astype(BF16)
    term = base("term", 3)
    gather_wait(2, sibling)
    gather_wait(2, diagonal)
    for i in range(2):
        target = i * 2 + 1 - core
        send(term_send.at[target], term_recv.at[i], term + i, {"ch": sibling})
    start, size = parts[2]
    level0[FWD_LEFT + start : FWD_LEFT + start + size, :] = project(2, w_in_ref).astype(BF16).astype(F32)
    gate_pre[start : start + size, :] = project(2, w_gate_ref)

    loads["conv_w"].wait()
    loads["gain"].wait()
    arrived(halo_recv.at[pl.ds(0, FWD_LEFT)], halo)
    arrived(halo_recv.at[pl.ds(FWD_LEFT, FWD_RIGHT)], halo + 1)
    own = FWD_LEFT + rows
    level0[0:FWD_LEFT, :] = halo_recv[0:FWD_LEFT, :].astype(F32) * left_live
    level0[own : own + FWD_RIGHT, :] = halo_recv[FWD_LEFT : FWD_LEFT + FWD_RIGHT, :].astype(F32) * right_live

    def convolve(source, level, sign, lo, hi, live, store):
        dilation = DILATIONS[level]
        for start, size in pieces(lo, hi):
            total = jnp.zeros((size, width), F32)
            for t in range(4):
                begin = start + sign * (t - 2) * dilation
                total = total + conv_w_ref[level, t : t + 1, :] * source[begin : begin + size, :]
            if live is not None:
                total = total * live
            store(start, size, total.astype(BF16).astype(F32))

    def into(target):
        def store(start, size, value):
            target[start : start + size, :] = value
        return store

    for level, (source, target) in enumerate(((level0, level1), (level1, level2))):
        lo, hi = ((8, own + 72), (24, own + 64))[level]
        convolve(source, level, 1, lo, FWD_LEFT, left_live, into(target))
        convolve(source, level, 1, FWD_LEFT, own, None, into(target))
        convolve(source, level, 1, own, hi, right_live, into(target))

    def store_gated(start, size, value):
        start = start - FWD_LEFT
        level3[start : start + size, :] = value
        gate = gate_pre[start : start + size, :]
        gated[start : start + size, :] = (value * (gate * jax.nn.sigmoid(gate))).astype(BF16)

    convolve(level2, 2, 1, FWD_LEFT, own, None, store_gated)

    mix = base("mix", 2 * groups)
    for q in range(groups):
        send(
            gated.at[pl.ds(rows - eighth - q * eighth, eighth)], both.at[ch, pl.ds(eighth, eighth)],
            mix + groups + ch, {"seq": mirror, "ch": q},
        )
    for d in range(1, groups):
        q = lax.rem(ch + d, groups)
        send(gated.at[top(q)], both.at[ch, pl.ds(0, eighth)], mix + ch, {"ch": q})
    both[ch, 0:eighth, :] = gated[top(ch), :]

    for i in range(2):
        arrived(term_recv.at[i], term + i)
    term_send[across] = (term_send[across].astype(F32) + term_recv[1 - x_lo].astype(F32)).astype(BF16)
    send(term_send.at[across], term_cross, term + 2, {"ch": across})
    arrived(term_cross, term + 2)
    grad_norm = term_send[ch].astype(F32) + term_recv[x_lo].astype(F32) + term_cross[...].astype(F32)
    scaled = grad_norm * gain_ref[...]

    for d in range(1, groups):
        q = lax.rem(ch + d, groups)
        arrived(both.at[q, pl.ds(0, eighth)], mix + q)
    for q in range(groups):
        arrived(both.at[q, pl.ds(eighth, eighth)], mix + groups + q)

    mine = jnp.concatenate([both[q] for q in range(groups)], axis=1)
    other = dot(flip, dot(mine, permute[...], (1, 0)).astype(BF16), (1, 0))
    combined = mine.astype(F32) + other
    inv_scale = lax.rsqrt(jnp.mean(combined * combined, axis=1, keepdims=True) + EPSILON)
    hat = combined * inv_scale
    normalized = (hat * gain_ref[...]).astype(BF16)
    norm_mix[top(ch), :] = normalized[:eighth]
    norm_mix[bottom(ch), :] = normalized[eighth:]
    row_total = jnp.sum(scaled * hat, axis=1, keepdims=True)
    grad_comb = (inv_scale * (scaled - hat * (row_total * (1.0 / full)))).astype(BF16)
    turned = dot(flip, dot(grad_comb, permute[...], (1, 1)).astype(BF16), (1, 0))
    returned = (grad_comb.astype(F32) + turned).astype(BF16)
    for q in range(groups):
        grad_split[q] = returned[:, q * width : (q + 1) * width]
    back = base("back", 2 * groups)
    for q in range(groups):
        send(
            grad_split.at[q, pl.ds(eighth, eighth)], grad_gated.at[bottom(ch)],
            back + groups + ch, {"seq": mirror, "ch": q},
        )
    for d in range(1, groups):
        q = lax.rem(ch + d, groups)
        send(grad_split.at[q, pl.ds(0, eighth)], grad_gated.at[top(ch)], back + ch, {"ch": q})
    grad_gated[top(ch), :] = grad_split[ch, 0:eighth, :]

    norm = base("norm", 2 * groups)

    def norm_send(q, target):
        send(norm_mix.at[top(q)], norm_mix.at[top(q)], norm + q, {"ch": target})
        send(norm_mix.at[bottom(q)], norm_mix.at[bottom(q)], norm + groups + q, {"ch": target})

    def norm_wait(q):
        arrived(norm_mix.at[top(q)], norm + q)
        arrived(norm_mix.at[bottom(q)], norm + groups + q)

    norm_send(ch, across)
    norm_send(ch, sibling)
    norm_wait(across)
    norm_send(across, sibling)

    conv_rows = 16
    size = full // ys
    part = size // zs
    names = ("out", "gate", "in")
    early, late = ("out", "gate"), ("in",)

    def span1(name):
        return pl.ds(0, size + (conv_rows if name == "in" else 0))

    def sem1(name, h, k):
        return base("sum " + name, 2 * ys) + h * ys + k

    def spread(name, value):
        g = names.index(name)
        for h in range(2):
            for k in range(first[h]):
                send1[g, h, k, 0:size, :] = value[k * size : (k + 1) * size, 128 * h : 128 * h + 128].astype(BF16)
        for d in range(1, ys):
            for h in range(2):
                t = lax.rem(me1[h] + d, first[h])
                send(
                    send1.at[g, h, t, span1(name)], recv1.at[g, h, me1[h], span1(name)],
                    sem1(name, h, me1[h]), first_peer(h, t),
                )

    def tall2(unit, same):
        return len(unit) * part + (conv_rows if same and unit is late else 0)

    def rows2(unit, same):
        return pl.ds(names.index(unit[0]) * part, tall2(unit, same))

    def sem2(unit, h, k):
        return base("over " + unit[0], 2 * xs * zs) + h * xs * zs + k

    def second_sum(unit):
        for h in range(2):
            for name in unit:
                g = names.index(name)
                total = send1[g, h, me1[h], 0:size, :].astype(F32)
                for d in range(1, first[h]):
                    k = lax.rem(me1[h] + d, first[h])
                    arrived(recv1.at[g, h, k, span1(name)], sem1(name, h, k))
                    total = total + recv1[g, h, k, 0:size, :].astype(F32)
                total = total.astype(BF16)
                for k in range(second[h]):
                    send2[h, k, g * part : (g + 1) * part, :] = total[k * part : (k + 1) * part]
            if unit is late:
                recv1[2, h, me1[h], size:, :] = send1[2, h, me1[h], size:, :]
                tail = jnp.zeros((conv_rows, 128), F32)
                for k in range(first[h]):
                    tail = tail + recv1[2, h, k, size:, :].astype(F32)
                for k in range(second[h]):
                    send2[h, k, 3 * part :, :] = tail.astype(BF16)
            slot = my_x * second[h] + me2[h]
            for dx in reversed(range(xs)):
                for dt in range(second[h]):
                    if dx or dt:
                        x = lax.rem(my_x + dx, xs)
                        t = lax.rem(me2[h] + dt, second[h])
                        span = rows2(unit, dx == 0)
                        send(send2.at[h, t, span], recv2.at[h, slot, span], sem2(unit, h, slot), second_peer(h, x, t))
            span = rows2(unit, True)
            recv2[h, slot, span, :] = send2[h, me2[h], span, :]

    def sem3(unit, h, k):
        return base("gather2 " + unit[0], 2 * zs) + h * zs + k

    conv_sem = base("conv", 2 * xs)

    def span3(unit):
        return pl.ds(names.index(unit[0]) * part, len(unit) * part)

    def second_gather(unit):
        for h in range(2):
            for dx in range(xs):
                for dt in range(second[h]):
                    if dx or dt:
                        k = lax.rem(my_x + dx, xs) * second[h] + lax.rem(me2[h] + dt, second[h])
                        arrived(recv2.at[h, k, rows2(unit, dx == 0)], sem2(unit, h, k))
            total = jnp.zeros((len(unit) * part, 128), F32)
            for k in range(xs * second[h]):
                total = total + recv2[h, k, span3(unit), :].astype(F32)
            whole[names.index(unit[0]) // 2, h, me1[h], me2[h], 0 : len(unit) * part] = total.astype(BF16)
            for d in range(1, second[h]):
                t = lax.rem(me2[h] + d, second[h])
                here = whole.at[names.index(unit[0]) // 2, h, me1[h], me2[h], pl.ds(0, len(unit) * part)]
                send(here, here, sem3(unit, h, me2[h]), second_peer(h, my_x, t))
            if unit is late:
                tail = jnp.zeros((conv_rows, 128), F32)
                for t in range(second[h]):
                    tail = tail + recv2[h, my_x * second[h] + t, 3 * part :, :].astype(F32)
                conv_x[h, my_x] = tail.astype(BF16)
                for dx in range(1, xs):
                    here = conv_x.at[h, my_x]
                    send(here, here, conv_sem + h * xs + my_x, at(lax.rem(my_x + dx, xs), my_z, my_y))

    def sem4(unit, h, k):
        return base("gather1 " + unit[0], 2 * ys) + h * ys + k

    def block4(unit, h, k):
        return whole.at[names.index(unit[0]) // 2, h, k, pl.ds(0, zs), pl.ds(0, len(unit) * part)]

    def first_gather(unit):
        u = names.index(unit[0]) // 2
        for h in range(2):
            for d in range(1, second[h]):
                k = lax.rem(me2[h] + d, second[h])
                arrived(whole.at[u, h, me1[h], k, pl.ds(0, len(unit) * part)], sem3(unit, h, k))
            for d in range(1, first[h]):
                t = lax.rem(me1[h] + d, first[h])
                send(block4(unit, h, me1[h]), block4(unit, h, me1[h]), sem4(unit, h, me1[h]), first_peer(h, t))

    outs = (grad_out_ref, grad_gate_ref, grad_in_ref)

    def place_rows(unit, h, k):
        for i, name in enumerate(unit):
            block = whole[names.index(unit[0]) // 2, h, k, :, i * part : (i + 1) * part, :]
            at_row = pl.multiple_of(k * size, size)
            outs[names.index(name)][pl.ds(at_row, size), 128 * h : 128 * h + 128] = block.reshape(size, 128)

    def finish(unit):
        for h in range(2):
            place_rows(unit, h, me1[h])
        for d in range(1, ys):
            for h in range(2):
                k = lax.rem(me1[h] + d, first[h])
                arrived(block4(unit, h, k), sem4(unit, h, k))
                place_rows(unit, h, k)

    for d in range(1, groups):
        q = lax.rem(ch + d, groups)
        arrived(grad_gated.at[top(q)], back + q)
    for q in range(groups):
        arrived(grad_gated.at[bottom(q)], back + groups + q)
    own = BWD_LEFT + rows
    for start, tall in pieces(0, rows):
        gate = gate_pre[start : start + tall, :]
        sigmoid = jax.nn.sigmoid(gate)
        grad = grad_gated[start : start + tall, :].astype(F32)
        upstream = (grad * (gate * sigmoid)).astype(BF16)
        up3_low[start : start + tall, :] = upstream
        up3[BWD_LEFT + start : BWD_LEFT + start + tall, :] = upstream.astype(F32)
        gate_low[start : start + tall, :] = (
            grad * level3[start : start + tall, :] * sigmoid * (1.0 + gate * (1.0 - sigmoid))
        ).astype(BF16)
    halo_back = base("halo_back", 2)
    send(up3_low.at[pl.ds(0, BWD_RIGHT)], halo_late.at[pl.ds(BWD_LEFT, BWD_RIGHT)], halo_back, {"seq": before})
    send(
        up3_low.at[pl.ds(rows - BWD_LEFT, BWD_LEFT)], halo_late.at[pl.ds(0, BWD_LEFT)], halo_back + 1, {"seq": after}
    )

    def against_input(value):
        return jnp.concatenate([dot(block_in[k], value, (0, 0)) for k in range(groups)], axis=0)

    norm_wait(sibling)
    norm_wait(diagonal)
    spread("out", dot(norm_mix[...], cot_mix[...], (0, 0)))
    spread("gate", against_input(gate_low[...]))

    arrived(halo_late.at[pl.ds(BWD_LEFT, BWD_RIGHT)], halo_back)
    arrived(halo_late.at[pl.ds(0, BWD_LEFT)], halo_back + 1)
    up3[0:BWD_LEFT, :] = halo_late[0:BWD_LEFT, :].astype(F32) * left_live
    up3[own : own + BWD_RIGHT, :] = halo_late[BWD_LEFT : BWD_LEFT + BWD_RIGHT, :].astype(F32) * right_live

    convolve(up3, 2, -1, 64, BWD_LEFT, left_live, into(up2))
    convolve(up3, 2, -1, BWD_LEFT, own, None, into(up2))
    convolve(up3, 2, -1, own, own + 24, right_live, into(up2))
    convolve(up2, 1, -1, 72, BWD_LEFT, left_live, into(up1))
    convolve(up2, 1, -1, BWD_LEFT, own, None, into(up1))
    convolve(up2, 1, -1, own, own + 8, right_live, into(up1))

    def store_last(start, tall, value):
        up0_low[start - BWD_LEFT : start - BWD_LEFT + tall, :] = value.astype(BF16)

    convolve(up1, 0, -1, BWD_LEFT, own, None, store_last)

    taps = []
    for level, (source, upstream) in enumerate(((level0, up1), (level1, up2), (level2, up3))):
        for t in range(4):
            total = jnp.zeros((8, width), F32)
            for start, tall in pieces(0, rows):
                begin = FWD_LEFT + start + (t - 2) * DILATIONS[level]
                term_product = (
                    upstream[BWD_LEFT + start : BWD_LEFT + start + tall, :] * source[begin : begin + tall, :]
                )
                total = total + jnp.sum(term_product.reshape(tall // 8, 8, width), axis=0)
            taps.append(jnp.sum(total, axis=0, keepdims=True))
    taps = jnp.concatenate(taps + [jnp.zeros((conv_rows - 12, width), F32)], axis=0).astype(BF16)
    for h in range(2):
        for k in range(first[h]):
            send1[2, h, k, size : size + conv_rows, :] = taps[:, 128 * h : 128 * h + 128]
    spread("in", against_input(up0_low[...]))

    second_sum(early)

    product = dot(norm_mix[...], w_out_ref[...], (1, 0))
    product_send[...] = product[half:].astype(BF16)
    product_sem = base("product", 1)
    send(product_send, product_recv, product_sem, {"seq": mirror})
    output_ref[0:half, :] = (block_in[ch, 0:half, :].astype(F32) + product[:half]).astype(BF16)
    store_out(output_ref.at[pl.ds(0, half)], output_out.at[pl.ds(0, half)])

    second_sum(late)
    second_gather(early)
    arrived(product_recv, product_sem)
    output_ref[half:rows, :] = (
        block_in[ch, half:rows, :].astype(F32) + product_recv[...].astype(F32)
    ).astype(BF16)
    store_out(output_ref.at[pl.ds(half, half)], output_out.at[pl.ds(half, half)])
    second_gather(late)
    first_gather(early)
    first_gather(late)
    for h in range(2):
        for dx in range(1, xs):
            x = lax.rem(my_x + dx, xs)
            arrived(conv_x.at[h, x], conv_sem + h * xs + x)
        tail = jnp.zeros((conv_rows, 128), F32)
        for x in range(xs):
            tail = tail + conv_x[h, x].astype(F32)
        for level in range(3):
            grad_conv_ref[level, :, 128 * h : 128 * h + 128] = tail[4 * level : 4 * level + 4]
    store_out(grad_conv_ref, grad_conv_out)
    finish(early)
    store_out(grad_out_ref, grad_out_out)
    store_out(grad_gate_ref, grad_gate_out)
    finish(late)
    store_out(grad_in_ref, grad_in_out)
    for copy in pending:
        copy.wait_send()
    for copy in stores:
        copy.wait()


def hand_over(*refs):
    count = len(refs) // 2
    sems = refs[-1]
    copies = [pltpu.make_async_copy(refs[i], refs[count + i], sems.at[i]) for i in range(count)]
    for copy in copies:
        copy.start()
    for copy in copies:
        copy.wait()


def local(tokens, hidden, embedding, w_in, w_gate, conv_w, channel_order, gain, w_out, cotangent):
    rows, width = hidden.shape
    full = gain.shape[0]
    groups = lax.axis_size("ch")
    sizes = ring_sizes(lax.axis_size("seq"))
    xs, zs, ys = sizes
    size = full // ys
    part = size // zs
    eighth = rows // (2 * groups)
    extended = rows + FWD_LEFT + FWD_RIGHT
    anywhere = pl.BlockSpec(memory_space=pl.ANY)
    dma = pltpu.SemaphoreType.DMA

    def held(*shape, dtype=BF16):
        return pltpu.VMEM(shape, dtype)

    weight = jax.ShapeDtypeStruct((full, width), BF16)
    results = (
        jax.ShapeDtypeStruct((rows, width), BF16), weight, weight, weight, jax.ShapeDtypeStruct((3, 4, width), F32)
    )
    computed = pl.pallas_call(
        functools.partial(block_kernel, sizes, groups),
        out_shape=results,
        in_specs=[anywhere] * 10,
        out_specs=(anywhere,) * 5,
        scratch_shapes=[
            held(1, rows, dtype=jnp.int32),
            held(rows, width),
            held(full, width),
            held(full, width),
            held(3, 4, width, dtype=F32),
            held(1, full, dtype=jnp.int32),
            held(1, full, dtype=F32),
            held(full, width),
            held(rows, width),
            held(full, width),
            held(full, width),
            held(full, width),
            held(3, 4, width, dtype=F32),
            held(groups, rows, width),
            held(16, width),
            held(extended, width, dtype=F32),
            held(extended, width, dtype=F32),
            held(extended, width, dtype=F32),
            held(rows, width, dtype=F32),
            held(rows, width, dtype=F32),
            held(FWD_LEFT + FWD_RIGHT, width),
            held(FWD_LEFT + FWD_RIGHT, width),
            held(BWD_LEFT + BWD_RIGHT, width),
            held(rows, width),
            held(groups, 2 * eighth, width),
            held(full, full),
            held(rows, width),
            held(groups, 2 * eighth, full),
            held(2, 2 * eighth, full),
            held(2 * eighth, full),
            held(rows, full),
            held(groups, 2 * eighth, width),
            held(rows, width),
            held(extended, width, dtype=F32),
            held(extended, width, dtype=F32),
            held(extended, width, dtype=F32),
            held(rows // 2, width),
            held(rows // 2, width),
            held(rows, width),
            held(rows, width),
            held(rows, width),
            held(3, 2, ys, size + 16, 128),
            held(3, 2, ys, size + 16, 128),
            held(2, zs, 3 * part + 16, 128),
            held(2, xs * zs, 3 * part + 16, 128),
            held(2, 2, ys, zs, 2 * part, 128),
            held(2, xs, 16, 128),
            dma((SENDS,)),
            dma((RECEIVES,)),
            dma((16,)),
        ],
        compiler_params=pltpu.CompilerParams(
            collective_id=0, has_side_effects=True, vmem_limit_bytes=56 * 1024 * 1024
        ),
    )(
        tokens.reshape(1, rows), hidden, embedding, w_in, w_gate, conv_w, channel_order.reshape(1, full),
        gain.reshape(1, full), w_out, cotangent,
    )
    return pl.pallas_call(
        hand_over,
        out_shape=results,
        in_specs=[anywhere] * 5,
        out_specs=(anywhere,) * 5,
        scratch_shapes=[dma((5,))],
        compiler_params=pltpu.CompilerParams(vmem_limit_bytes=60 * 1024 * 1024),
    )(*computed)


def solution(mesh):
    placed = (
        P("seq"),
        P("seq", "ch"),
        P(None, "ch"),
        P(None, "ch"),
        P(None, "ch"),
        P(None, None, "ch"),
        P(),
        P(),
        P(None, "ch"),
        P("seq", "ch"),
    )
    return jax.shard_map(
        local,
        mesh=mesh,
        in_specs=placed,
        out_specs=(
            P("seq", "ch"),
            P(None, "ch"),
            P(None, "ch"),
            P(None, "ch"),
            P(None, None, "ch"),
        ),
        check_vma=False,
    )
```

```python
import functools

import jax
import jax.numpy as jnp
from jax import lax
from jax.experimental import pallas as pl
from jax.experimental.pallas import tpu as pltpu
from jax.sharding import PartitionSpec as P

DILATIONS = (1, 8, 64)
EPSILON = 1e-06
MESH = pl.DeviceIdType.MESH
BF16 = jnp.bfloat16
F32 = jnp.float32

FWD_LEFT, FWD_RIGHT = 160, 80
BWD_LEFT, BWD_RIGHT = 80, 160
CHUNK = 64
SENDS = 128
RECEIVES = 160


def ring_sizes(count):
    return {128: (2, 8, 8), 8: (2, 2, 2), 4: (1, 2, 2)}[count]


def dot(a, b, contract):
    return lax.dot_general(a, b, ((contract[:1], contract[1:]), ((), ())), preferred_element_type=F32)


def pieces(lo, hi):
    return [(start, min(CHUNK, hi - start)) for start in range(lo, hi, CHUNK)]


def block_kernel(
    sizes, groups,
    tokens_in, hidden_in, embedding_in, w_in_in, w_gate_in, conv_w_in, order_in, gain_in, w_out_in, cot_in,
    output_out, grad_in_out, grad_gate_out, grad_out_out, grad_conv_out,
    tokens_ref, hidden_ref, w_in_ref, w_gate_ref, conv_w_ref, order_ref, gain_ref, w_out_ref,
    output_ref, grad_in_ref, grad_gate_ref, grad_out_ref, grad_conv_ref,
    block_in, embed, level0, level1, level2, level3, gate_pre, halo_send, halo_recv, halo_late,
    gated, both, permute, cot_near, cot_far, cot_mix, term_send, term_recv, term_cross, norm_mix, grad_split,
    grad_gated, up3, up2, up1, product_send, product_recv, up3_low, up0_low, gate_low,
    send1, recv1, send1_late, recv1_late, send2, recv2, whole, conv_x, send_sem, recv_sem, local_sem,
):
    xs, zs, ys = sizes
    count = xs * zs * ys
    rows, width = hidden_ref.shape
    full = width * groups
    eighth = rows // (2 * groups)
    half = rows // 2

    seq = lax.axis_index("seq")
    ch = lax.axis_index("ch")
    core = lax.rem(ch, 2)
    x_lo = lax.div(ch, 2)
    sibling = x_lo * 2 + 1 - core
    across = (1 - x_lo) * 2 + core
    diagonal = (1 - x_lo) * 2 + 1 - core
    mirror = count - 1 - seq
    after = lax.rem(seq + 1, count)
    before = lax.rem(seq + count - 1, count)
    my_y = lax.rem(seq, ys)
    my_z = lax.rem(lax.div(seq, ys), zs)
    my_x = lax.div(seq, ys * zs)
    left_live = (seq > 0).astype(F32)
    right_live = (seq < count - 1).astype(F32)

    def at(x, z, y):
        return {"seq": (x * zs + z) * ys + y}

    assert ys == zs
    ring = ys
    me1 = my_y + core * (my_z - my_y)
    me2 = my_z + core * (my_y - my_z)

    def first_peer(t):
        return at(my_x, my_z + core * (t - my_z), t + core * (my_y - t))

    def second_peer(x, t):
        return at(x, t + core * (my_z - t), my_y + core * (t - my_y))

    def top(q):
        return pl.ds(pl.multiple_of(q * eighth, eighth), eighth)

    def bottom(q):
        return pl.ds(pl.multiple_of(rows - eighth - q * eighth, eighth), eighth)

    barrier = pltpu.get_barrier_semaphore()
    greeted = []

    def greet(device):
        pl.semaphore_signal(barrier, inc=1, device_id=device, device_id_type=MESH)
        greeted.append(0)

    greet({"ch": sibling})
    greet({"ch": across})
    greet({"ch": diagonal})
    for q in range(groups):
        greet({"seq": mirror, "ch": q})
    greet({"seq": after})
    greet({"seq": before})
    for d in range(1, ring):
        greet(first_peer(lax.rem(me1 + d, ring)))
    for dx in range(xs):
        for d in range(ring):
            if dx or d:
                greet(second_peer(lax.rem(my_x + dx, xs), lax.rem(me2 + d, ring)))

    pending = []
    bases = {}

    def base(name, size):
        if name not in bases:
            bases[name] = sum(taken for _, taken in bases.values()), size
        return bases[name][0]

    def send(src, dst, receive, device):
        copy = pltpu.make_async_remote_copy(
            src_ref=src, dst_ref=dst, send_sem=send_sem.at[len(pending)], recv_sem=recv_sem.at[receive],
            device_id=device, device_id_type=MESH,
        )
        copy.start()
        pending.append(copy)

    def arrived(dst, receive):
        pltpu.make_async_remote_copy(
            src_ref=dst, dst_ref=dst, send_sem=send_sem.at[0], recv_sem=recv_sem.at[receive],
            device_id={"ch": sibling}, device_id_type=MESH,
        ).wait_recv()

    embed[...] = jnp.zeros_like(embed)
    loads = {}
    for name, src, dst in (
        ("tokens", tokens_in, tokens_ref),
        ("embedding", embedding_in, embed.at[pl.ds(0, 4)]),
        ("hidden", hidden_in, hidden_ref),
        ("cot", cot_in.at[pl.ds(0, half)], cot_near),
        ("order", order_in, order_ref),
        ("w_in", w_in_in, w_in_ref),
        ("w_gate", w_gate_in, w_gate_ref),
        ("w_out", w_out_in, w_out_ref),
        ("conv_w", conv_w_in, conv_w_ref),
        ("gain", gain_in, gain_ref),
    ):
        loads[name] = pltpu.make_async_copy(src, dst, local_sem.at[len(loads)])
        loads[name].start()
    stores = []

    def store_out(src, dst):
        copy = pltpu.make_async_copy(src, dst, local_sem.at[len(loads) + len(stores)])
        copy.start()
        stores.append(copy)

    for name in ("tokens", "embedding", "hidden"):
        loads[name].wait()
    hot = (lax.broadcasted_iota(jnp.int32, (16, rows), 0) == tokens_ref[...]).astype(F32).astype(BF16)
    looked_up = dot(hot, embed[...], (0, 0))
    block_in[ch] = (hidden_ref[...].astype(F32) + looked_up).astype(BF16)

    pl.semaphore_wait(barrier, len(greeted))

    parts = ((rows - FWD_LEFT, FWD_LEFT), (0, FWD_RIGHT), (FWD_RIGHT, rows - FWD_LEFT - FWD_RIGHT))
    gather = base("gather", 3 * groups)

    def gather_part(i, slot):
        return block_in.at[slot, pl.ds(parts[i][0], parts[i][1])]

    def gather_send(i, slot, target):
        send(gather_part(i, slot), gather_part(i, slot), gather + i * groups + slot, {"ch": target})

    def gather_wait(i, slot):
        arrived(gather_part(i, slot), gather + i * groups + slot)

    for i in range(3):
        gather_send(i, ch, across)
    send(block_in.at[ch], block_in.at[ch], gather + ch, {"ch": sibling})
    cot_sem = base("cot", 1)
    send(cot_in.at[pl.ds(half, half)], cot_far, cot_sem, {"seq": mirror})

    loads["order"].wait()
    for start in range(0, full, 128):
        place = lax.broadcasted_iota(jnp.int32, (128, full), 0) + start
        permute[start : start + 128, :] = (place == order_ref[...]).astype(F32).astype(BF16)
    flip = (
        lax.broadcasted_iota(jnp.int32, (2 * eighth, 2 * eighth), 0)
        + lax.broadcasted_iota(jnp.int32, (2 * eighth, 2 * eighth), 1)
        == 2 * eighth - 1
    ).astype(F32).astype(BF16)

    def terms(source, part):
        value = dot(source[...], w_out_ref[...], (1, 1)).astype(BF16)
        for q in range(groups):
            start = q * eighth if part == 0 else half - eighth - q * eighth
            span = slice(part * eighth, (part + 1) * eighth)
            term_send[q, span, :] = value[start : start + eighth]
            cot_mix[q, span, :] = source[start : start + eighth, :]

    loads["cot"].wait()
    loads["w_out"].wait()
    terms(cot_near, 0)

    def project(i, weights):
        start, size = parts[i]
        total = jnp.zeros((size, width), F32)
        for k in range(groups):
            total = total + dot(block_in[k, start : start + size, :], weights[k * width : (k + 1) * width, :], (1, 0))
        return total

    loads["w_in"].wait()
    halo = base("halo", 2)
    for i in range(2):
        gather_wait(i, across)
        gather_send(i, across, sibling)
    for i in range(2):
        start, size = parts[i]
        if i == 0:
            arrived(block_in.at[sibling], gather + sibling)
        gather_wait(i, diagonal)
        projected = project(i, w_in_ref).astype(BF16)
        level0[FWD_LEFT + start : FWD_LEFT + start + size, :] = projected.astype(F32)
        keep = pl.ds(0, FWD_LEFT) if i == 0 else pl.ds(FWD_LEFT, FWD_RIGHT)
        halo_send[keep, :] = projected
        send(halo_send.at[keep], halo_recv.at[keep], halo + i, {"seq": after if i == 0 else before})
    gather_wait(2, across)
    gather_send(2, across, sibling)
    loads["w_gate"].wait()
    for i in range(2):
        start, size = parts[i]
        gate_pre[start : start + size, :] = project(i, w_gate_ref)

    arrived(cot_far, cot_sem)
    terms(cot_far, 1)
    term = base("term", 3)
    gather_wait(2, diagonal)
    for i in range(2):
        target = i * 2 + 1 - core
        send(term_send.at[target], term_recv.at[i], term + i, {"ch": sibling})
    start, size = parts[2]
    level0[FWD_LEFT + start : FWD_LEFT + start + size, :] = project(2, w_in_ref).astype(BF16).astype(F32)
    gate_pre[start : start + size, :] = project(2, w_gate_ref)

    loads["conv_w"].wait()
    loads["gain"].wait()
    arrived(halo_recv.at[pl.ds(0, FWD_LEFT)], halo)
    arrived(halo_recv.at[pl.ds(FWD_LEFT, FWD_RIGHT)], halo + 1)
    own = FWD_LEFT + rows
    level0[0:FWD_LEFT, :] = halo_recv[0:FWD_LEFT, :].astype(F32) * left_live
    level0[own : own + FWD_RIGHT, :] = halo_recv[FWD_LEFT : FWD_LEFT + FWD_RIGHT, :].astype(F32) * right_live

    def convolve(source, level, sign, lo, hi, live, store):
        dilation = DILATIONS[level]
        for start, size in pieces(lo, hi):
            total = jnp.zeros((size, width), F32)
            for t in range(4):
                begin = start + sign * (t - 2) * dilation
                total = total + conv_w_ref[level, t : t + 1, :] * source[begin : begin + size, :]
            if live is not None:
                total = total * live
            store(start, size, total.astype(BF16).astype(F32))

    def into(target):
        def store(start, size, value):
            target[start : start + size, :] = value
        return store

    for level, (source, target) in enumerate(((level0, level1), (level1, level2))):
        lo, hi = ((8, own + 72), (24, own + 64))[level]
        convolve(source, level, 1, lo, FWD_LEFT, left_live, into(target))
        convolve(source, level, 1, FWD_LEFT, own, None, into(target))
        convolve(source, level, 1, own, hi, right_live, into(target))

    def store_gated(start, size, value):
        start = start - FWD_LEFT
        level3[start : start + size, :] = value
        gate = gate_pre[start : start + size, :]
        gated[start : start + size, :] = (value * (gate * jax.nn.sigmoid(gate))).astype(BF16)

    convolve(level2, 2, 1, FWD_LEFT, own, None, store_gated)

    mix = base("mix", 2 * groups)
    for q in range(groups):
        send(
            gated.at[pl.ds(rows - eighth - q * eighth, eighth)], both.at[ch, pl.ds(eighth, eighth)],
            mix + groups + ch, {"seq": mirror, "ch": q},
        )
    for d in range(1, groups):
        q = lax.rem(ch + d, groups)
        send(gated.at[top(q)], both.at[ch, pl.ds(0, eighth)], mix + ch, {"ch": q})
    both[ch, 0:eighth, :] = gated[top(ch), :]

    for i in range(2):
        arrived(term_recv.at[i], term + i)
    term_send[across] = (term_send[across].astype(F32) + term_recv[1 - x_lo].astype(F32)).astype(BF16)
    send(term_send.at[across], term_cross, term + 2, {"ch": across})
    arrived(term_cross, term + 2)
    grad_norm = term_send[ch].astype(F32) + term_recv[x_lo].astype(F32) + term_cross[...].astype(F32)
    scaled = grad_norm * gain_ref[...]

    for d in range(1, groups):
        q = lax.rem(ch + d, groups)
        arrived(both.at[q, pl.ds(0, eighth)], mix + q)
    for q in range(groups):
        arrived(both.at[q, pl.ds(eighth, eighth)], mix + groups + q)

    mine = jnp.concatenate([both[q] for q in range(groups)], axis=1)
    other = dot(flip, dot(mine, permute[...], (1, 0)).astype(BF16), (1, 0))
    combined = mine.astype(F32) + other
    inv_scale = lax.rsqrt(jnp.mean(combined * combined, axis=1, keepdims=True) + EPSILON)
    hat = combined * inv_scale
    normalized = (hat * gain_ref[...]).astype(BF16)
    norm_mix[ch] = normalized
    row_total = jnp.sum(scaled * hat, axis=1, keepdims=True)
    grad_comb = (inv_scale * (scaled - hat * (row_total * (1.0 / full)))).astype(BF16)
    turned = dot(flip, dot(grad_comb, permute[...], (1, 1)).astype(BF16), (1, 0))
    returned = (grad_comb.astype(F32) + turned).astype(BF16)
    for q in range(groups):
        grad_split[q] = returned[:, q * width : (q + 1) * width]
    back = base("back", 2 * groups)
    for q in range(groups):
        send(
            grad_split.at[q, pl.ds(eighth, eighth)], grad_gated.at[bottom(ch)],
            back + groups + ch, {"seq": mirror, "ch": q},
        )
    for d in range(1, groups):
        q = lax.rem(ch + d, groups)
        send(grad_split.at[q, pl.ds(0, eighth)], grad_gated.at[top(ch)], back + ch, {"ch": q})
    grad_gated[top(ch), :] = grad_split[ch, 0:eighth, :]

    norm = base("norm", groups)

    def norm_send(q, target):
        send(norm_mix.at[q], norm_mix.at[q], norm + q, {"ch": target})

    def norm_wait(q):
        arrived(norm_mix.at[q], norm + q)

    norm_send(ch, across)
    norm_send(ch, sibling)
    norm_wait(across)
    norm_send(across, sibling)

    conv_rows = 16
    size = full // ring
    part = size // ring
    early, late = (0, 2), (2, 1)
    first_send = {early: send1, late: send1_late}
    first_recv = {early: recv1, late: recv1_late}

    def spread(unit, values):
        for k in range(ring):
            for g, value in enumerate(values):
                first_send[unit][k, g * size : (g + 1) * size, :] = value[k * size : (k + 1) * size].astype(BF16)
        for d in range(1, ring):
            t = lax.rem(me1 + d, ring)
            send(first_send[unit].at[t], first_recv[unit].at[me1], sem1(unit, me1), first_peer(t))

    def sem1(unit, k):
        return base(("sum", unit), ring) + k

    def rows2(unit, same):
        return pl.ds(unit[0] * part, unit[1] * part + (conv_rows if same and unit is late else 0))

    def sem2(unit, k):
        return base(("over", unit), xs * ring) + k

    def second_sum(unit):
        tall = unit[1] * size
        total = first_send[unit][me1, 0:tall, :].astype(F32)
        for d in range(1, ring):
            k = lax.rem(me1 + d, ring)
            arrived(first_recv[unit].at[k], sem1(unit, k))
            total = total + first_recv[unit][k, 0:tall, :].astype(F32)
        total = total.astype(BF16)
        for k in range(ring):
            for g in range(unit[1]):
                low = (unit[0] + g) * part
                send2[k, low : low + part, :] = total[g * size + k * part : g * size + (k + 1) * part]
        if unit is late:
            recv1_late[me1, size:, :] = send1_late[me1, size:, :]
            tail = jnp.zeros((conv_rows, width), F32)
            for k in range(ring):
                tail = tail + recv1_late[k, size:, :].astype(F32)
            for k in range(ring):
                send2[k, 3 * part :, :] = tail.astype(BF16)
        slot = my_x * ring + me2
        for dx in reversed(range(xs)):
            for d in range(ring):
                if dx or d:
                    x = lax.rem(my_x + dx, xs)
                    t = lax.rem(me2 + d, ring)
                    span = rows2(unit, dx == 0)
                    send(send2.at[t, span], recv2.at[slot, span], sem2(unit, slot), second_peer(x, t))
        span = rows2(unit, True)
        recv2[slot, span, :] = send2[me2, span, :]

    def sem3(unit, k):
        return base(("gather2", unit), ring) + k

    def sem4(unit, k):
        return base(("gather1", unit), ring) + k

    conv_sem = base("conv", xs)

    def finished(unit, k, m=None):
        if unit is late:
            if m is None:
                return grad_in_ref.at[pl.ds(pl.multiple_of(k * size, size), size)]
            return grad_in_ref.at[pl.ds(pl.multiple_of(k * size + m * part, part), part)]
        return whole.at[k] if m is None else whole.at[k, m]

    def second_gather(unit):
        for dx in range(xs):
            for d in range(ring):
                if dx or d:
                    k = lax.rem(my_x + dx, xs) * ring + lax.rem(me2 + d, ring)
                    arrived(recv2.at[k, rows2(unit, dx == 0)], sem2(unit, k))
        span = rows2(unit, False)
        total = jnp.zeros((unit[1] * part, width), F32)
        for k in range(xs * ring):
            total = total + recv2[k, span, :].astype(F32)
        here = finished(unit, me1, me2)
        here[...] = total.astype(BF16)
        for d in range(1, ring):
            send(here, here, sem3(unit, me2), second_peer(my_x, lax.rem(me2 + d, ring)))
        if unit is late:
            tail = jnp.zeros((conv_rows, width), F32)
            for t in range(ring):
                tail = tail + recv2[my_x * ring + t, 3 * part :, :].astype(F32)
            conv_x[my_x] = tail.astype(BF16)
            for dx in range(1, xs):
                here = conv_x.at[my_x]
                send(here, here, conv_sem + my_x, at(lax.rem(my_x + dx, xs), my_z, my_y))

    def first_gather(unit):
        for d in range(1, ring):
            k = lax.rem(me2 + d, ring)
            arrived(finished(unit, me1, k), sem3(unit, k))
        here = finished(unit, me1)
        for d in range(1, ring):
            send(here, here, sem4(unit, me1), first_peer(lax.rem(me1 + d, ring)))

    def finish(unit):
        for d in range(1, ring):
            k = lax.rem(me1 + d, ring)
            arrived(finished(unit, k), sem4(unit, k))

    for d in range(1, groups):
        q = lax.rem(ch + d, groups)
        arrived(grad_gated.at[top(q)], back + q)
    for q in range(groups):
        arrived(grad_gated.at[bottom(q)], back + groups + q)
    own = BWD_LEFT + rows
    for start, tall in pieces(0, rows):
        gate = gate_pre[start : start + tall, :]
        sigmoid = jax.nn.sigmoid(gate)
        grad = grad_gated[start : start + tall, :].astype(F32)
        upstream = (grad * (gate * sigmoid)).astype(BF16)
        up3_low[start : start + tall, :] = upstream
        up3[BWD_LEFT + start : BWD_LEFT + start + tall, :] = upstream.astype(F32)
        gate_low[start : start + tall, :] = (
            grad * level3[start : start + tall, :] * sigmoid * (1.0 + gate * (1.0 - sigmoid))
        ).astype(BF16)
    halo_back = base("halo_back", 2)
    send(up3_low.at[pl.ds(0, BWD_RIGHT)], halo_late.at[pl.ds(BWD_LEFT, BWD_RIGHT)], halo_back, {"seq": before})
    send(
        up3_low.at[pl.ds(rows - BWD_LEFT, BWD_LEFT)], halo_late.at[pl.ds(0, BWD_LEFT)], halo_back + 1, {"seq": after}
    )

    def against_input(value):
        return jnp.concatenate([dot(block_in[k], value, (0, 0)) for k in range(groups)], axis=0)

    norm_wait(sibling)
    norm_wait(diagonal)
    normalized_rows = norm_mix[...].reshape(rows, full)
    spread(early, (dot(normalized_rows, cot_mix[...].reshape(rows, width), (0, 0)), against_input(gate_low[...])))

    arrived(halo_late.at[pl.ds(BWD_LEFT, BWD_RIGHT)], halo_back)
    arrived(halo_late.at[pl.ds(0, BWD_LEFT)], halo_back + 1)
    up3[0:BWD_LEFT, :] = halo_late[0:BWD_LEFT, :].astype(F32) * left_live
    up3[own : own + BWD_RIGHT, :] = halo_late[BWD_LEFT : BWD_LEFT + BWD_RIGHT, :].astype(F32) * right_live

    convolve(up3, 2, -1, 64, BWD_LEFT, left_live, into(up2))
    convolve(up3, 2, -1, BWD_LEFT, own, None, into(up2))
    convolve(up3, 2, -1, own, own + 24, right_live, into(up2))
    convolve(up2, 1, -1, 72, BWD_LEFT, left_live, into(up1))
    convolve(up2, 1, -1, BWD_LEFT, own, None, into(up1))
    convolve(up2, 1, -1, own, own + 8, right_live, into(up1))

    def store_last(start, tall, value):
        up0_low[start - BWD_LEFT : start - BWD_LEFT + tall, :] = value.astype(BF16)

    convolve(up1, 0, -1, BWD_LEFT, own, None, store_last)

    taps = []
    for level, (source, upstream) in enumerate(((level0, up1), (level1, up2), (level2, up3))):
        for t in range(4):
            total = jnp.zeros((8, width), F32)
            for start, tall in pieces(0, rows):
                begin = FWD_LEFT + start + (t - 2) * DILATIONS[level]
                term_product = (
                    upstream[BWD_LEFT + start : BWD_LEFT + start + tall, :] * source[begin : begin + tall, :]
                )
                total = total + jnp.sum(term_product.reshape(tall // 8, 8, width), axis=0)
            taps.append(jnp.sum(total, axis=0, keepdims=True))
    taps = jnp.concatenate(taps + [jnp.zeros((conv_rows - 12, width), F32)], axis=0).astype(BF16)
    for k in range(ring):
        send1_late[k, size : size + conv_rows, :] = taps
    spread(late, (against_input(up0_low[...]),))

    second_sum(early)

    product = dot(norm_mix[...].reshape(rows, full), w_out_ref[...], (1, 0))
    for q in range(groups):
        near = product[q * 2 * eighth : q * 2 * eighth + eighth]
        low = q * eighth
        output_ref[low : low + eighth, :] = (block_in[ch, low : low + eighth, :].astype(F32) + near).astype(BF16)
        low = half - eighth - q * eighth
        product_send[low : low + eighth, :] = product[q * 2 * eighth + eighth : (q + 1) * 2 * eighth].astype(BF16)
    product_sem = base("product", 1)
    send(product_send, product_recv, product_sem, {"seq": mirror})
    store_out(output_ref.at[pl.ds(0, half)], output_out.at[pl.ds(0, half)])

    second_sum(late)
    second_gather(early)
    arrived(product_recv, product_sem)
    output_ref[half:rows, :] = (
        block_in[ch, half:rows, :].astype(F32) + product_recv[...].astype(F32)
    ).astype(BF16)
    store_out(output_ref.at[pl.ds(half, half)], output_out.at[pl.ds(half, half)])
    second_gather(late)
    first_gather(early)
    first_gather(late)
    for dx in range(1, xs):
        x = lax.rem(my_x + dx, xs)
        arrived(conv_x.at[x], conv_sem + x)
    tail = jnp.zeros((conv_rows, width), F32)
    for x in range(xs):
        tail = tail + conv_x[x].astype(F32)
    for level in range(3):
        grad_conv_ref[level] = tail[4 * level : 4 * level + 4]
    store_out(grad_conv_ref, grad_conv_out)
    finish(early)
    for k in range(ring):
        for g, target in enumerate((grad_out_ref, grad_gate_ref)):
            target[k * size : (k + 1) * size, :] = whole[k, :, g * part : (g + 1) * part, :].reshape(size, width)
    store_out(grad_out_ref, grad_out_out)
    store_out(grad_gate_ref, grad_gate_out)
    finish(late)
    store_out(grad_in_ref, grad_in_out)
    for copy in pending:
        copy.wait_send()
    for copy in stores:
        copy.wait()


def hand_over(*refs):
    count = len(refs) // 3
    given, results, stages, sems = refs[:count], refs[count : 2 * count], refs[2 * count : 3 * count], refs[-1]
    loads = [pltpu.make_async_copy(given[i], stages[i], sems.at[0, i]) for i in range(count)]
    stores = [pltpu.make_async_copy(stages[i], results[i], sems.at[1, i]) for i in range(count)]
    for copy in loads:
        copy.start()
    for load, store in zip(loads, stores):
        load.wait()
        store.start()
    for copy in stores:
        copy.wait()


def local(tokens, hidden, embedding, w_in, w_gate, conv_w, channel_order, gain, w_out, cotangent):
    rows, width = hidden.shape
    full = gain.shape[0]
    groups = lax.axis_size("ch")
    sizes = ring_sizes(lax.axis_size("seq"))
    xs, zs, ys = sizes
    size = full // ys
    part = size // zs
    eighth = rows // (2 * groups)
    extended = rows + FWD_LEFT + FWD_RIGHT
    anywhere = pl.BlockSpec(memory_space=pl.ANY)
    dma = pltpu.SemaphoreType.DMA

    def held(*shape, dtype=BF16):
        return pltpu.VMEM(shape, dtype)

    weight = jax.ShapeDtypeStruct((full, width), BF16)
    results = (
        jax.ShapeDtypeStruct((rows, width), BF16), weight, weight, weight, jax.ShapeDtypeStruct((3, 4, width), F32)
    )
    computed = pl.pallas_call(
        functools.partial(block_kernel, sizes, groups),
        out_shape=results,
        in_specs=[anywhere] * 10,
        out_specs=(anywhere,) * 5,
        scratch_shapes=[
            held(1, rows, dtype=jnp.int32),
            held(rows, width),
            held(full, width),
            held(full, width),
            held(3, 4, width, dtype=F32),
            held(1, full, dtype=jnp.int32),
            held(1, full, dtype=F32),
            held(full, width),
            held(rows, width),
            held(full, width),
            held(full, width),
            held(full, width),
            held(3, 4, width, dtype=F32),
            held(groups, rows, width),
            held(16, width),
            held(extended, width, dtype=F32),
            held(extended, width, dtype=F32),
            held(extended, width, dtype=F32),
            held(rows, width, dtype=F32),
            held(rows, width, dtype=F32),
            held(FWD_LEFT + FWD_RIGHT, width),
            held(FWD_LEFT + FWD_RIGHT, width),
            held(BWD_LEFT + BWD_RIGHT, width),
            held(rows, width),
            held(groups, 2 * eighth, width),
            held(full, full),
            held(rows // 2, width),
            held(rows // 2, width),
            held(groups, 2 * eighth, width),
            held(groups, 2 * eighth, full),
            held(2, 2 * eighth, full),
            held(2 * eighth, full),
            held(groups, 2 * eighth, full),
            held(groups, 2 * eighth, width),
            held(rows, width),
            held(extended, width, dtype=F32),
            held(extended, width, dtype=F32),
            held(extended, width, dtype=F32),
            held(rows // 2, width),
            held(rows // 2, width),
            held(rows, width),
            held(rows, width),
            held(rows, width),
            held(ys, 2 * size, width),
            held(ys, 2 * size, width),
            held(ys, size + 16, width),
            held(ys, size + 16, width),
            held(zs, 3 * part + 16, width),
            held(xs * zs, 3 * part + 16, width),
            held(ys, zs, 2 * part, width),
            held(xs, 16, width),
            dma((SENDS,)),
            dma((RECEIVES,)),
            dma((16,)),
        ],
        compiler_params=pltpu.CompilerParams(
            collective_id=0, has_side_effects=True, vmem_limit_bytes=56 * 1024 * 1024
        ),
    )(
        tokens.reshape(1, rows), hidden, embedding, w_in, w_gate, conv_w, channel_order.reshape(1, full),
        gain.reshape(1, full), w_out, cotangent,
    )
    return pl.pallas_call(
        hand_over,
        out_shape=results,
        in_specs=[anywhere] * 5,
        out_specs=(anywhere,) * 5,
        scratch_shapes=[held(*result.shape, dtype=result.dtype) for result in results] + [dma((2, 5))],
        compiler_params=pltpu.CompilerParams(vmem_limit_bytes=60 * 1024 * 1024),
    )(*computed)


def solution(mesh):
    placed = (
        P("seq"),
        P("seq", "ch"),
        P(None, "ch"),
        P(None, "ch"),
        P(None, "ch"),
        P(None, None, "ch"),
        P(),
        P(),
        P(None, "ch"),
        P("seq", "ch"),
    )
    return jax.shard_map(
        local,
        mesh=mesh,
        in_specs=placed,
        out_specs=(
            P("seq", "ch"),
            P(None, "ch"),
            P(None, "ch"),
            P(None, "ch"),
            P(None, None, "ch"),
        ),
        check_vma=False,
    )
```

```python
import functools

import jax
import jax.numpy as jnp
from jax import lax
from jax.experimental import pallas as pl
from jax.experimental.pallas import tpu as pltpu
from jax.sharding import PartitionSpec as P

DILATIONS = (1, 8, 64)
EPSILON = 1e-06
MESH = pl.DeviceIdType.MESH
BF16 = jnp.bfloat16
F32 = jnp.float32

FWD_LEFT, FWD_RIGHT = 160, 80
BWD_LEFT, BWD_RIGHT = 80, 160
CHUNK = 64
SENDS = 272
RECEIVES = 304


def ring_sizes(count):
    return {128: (2, 8, 8), 8: (2, 2, 2), 4: (1, 2, 2)}[count]


def dot(a, b, contract):
    return lax.dot_general(a, b, ((contract[:1], contract[1:]), ((), ())), preferred_element_type=F32)


def pieces(lo, hi):
    return [(start, min(CHUNK, hi - start)) for start in range(lo, hi, CHUNK)]


def block_kernel(
    sizes, groups,
    tokens_in, hidden_in, embedding_in, w_in_in, w_gate_in, conv_w_in, order_in, gain_in, w_out_in, cot_in,
    output_out, grad_in_out, grad_gate_out, grad_out_out, grad_conv_out,
    tokens_ref, hidden_ref, w_in_ref, w_gate_ref, conv_w_ref, order_ref, gain_ref, w_out_ref,
    output_ref, grad_in_ref, grad_gate_ref, grad_out_ref, grad_conv_ref,
    block_in, embed, level0, level1, level2, level3, gate_pre, halo_send, halo_recv, halo_late,
    gated, both, permute, cot_near, cot_far, cot_mix, term_send, term_recv, term_cross, norm_mix, grad_split,
    grad_gated, up3, up2, up1, product_send, product_recv, up3_low, up0_low, gate_low,
    send1, recv1, send2, recv2, conv_x, send_sem, recv_sem, local_sem,
):
    xs, zs, ys = sizes
    count = xs * zs * ys
    rows, width = hidden_ref.shape
    full = width * groups
    eighth = rows // (2 * groups)
    half = rows // 2

    seq = lax.axis_index("seq")
    ch = lax.axis_index("ch")
    core = lax.rem(ch, 2)
    x_lo = lax.div(ch, 2)
    sibling = x_lo * 2 + 1 - core
    across = (1 - x_lo) * 2 + core
    diagonal = (1 - x_lo) * 2 + 1 - core
    mirror = count - 1 - seq
    after = lax.rem(seq + 1, count)
    before = lax.rem(seq + count - 1, count)
    my_y = lax.rem(seq, ys)
    my_z = lax.rem(lax.div(seq, ys), zs)
    my_x = lax.div(seq, ys * zs)
    left_live = (seq > 0).astype(F32)
    right_live = (seq < count - 1).astype(F32)

    def at(x, z, y):
        return {"seq": (x * zs + z) * ys + y}

    assert ys == zs
    ring = ys
    me1 = (my_y, my_z)
    me2 = (my_z, my_y)

    def first_peer(h, t):
        return at(my_x, my_z, t) if h == 0 else at(my_x, t, my_y)

    def second_peer(h, x, t):
        return at(x, t, my_y) if h == 0 else at(x, my_z, t)

    def top(q):
        return pl.ds(pl.multiple_of(q * eighth, eighth), eighth)

    def bottom(q):
        return pl.ds(pl.multiple_of(rows - eighth - q * eighth, eighth), eighth)

    barrier = pltpu.get_barrier_semaphore()
    greeted = []

    def greet(device):
        pl.semaphore_signal(barrier, inc=1, device_id=device, device_id_type=MESH)
        greeted.append(0)

    greet({"ch": sibling})
    greet({"ch": across})
    greet({"ch": diagonal})
    for q in range(groups):
        greet({"seq": mirror, "ch": q})
    greet({"seq": after})
    greet({"seq": before})
    for h in range(2):
        for d in range(1, ring):
            greet(first_peer(h, lax.rem(me1[h] + d, ring)))
    for dx in range(1, xs):
        x = lax.rem(my_x + dx, xs)
        for d in range(ring):
            greet(second_peer(0, x, lax.rem(my_z + d, ring)))
        for d in range(1, ring):
            greet(second_peer(1, x, lax.rem(my_y + d, ring)))

    pending = []
    bases = {}

    def base(name, size):
        if name not in bases:
            bases[name] = sum(taken for _, taken in bases.values()), size
        return bases[name][0]

    def send(src, dst, receive, device):
        copy = pltpu.make_async_remote_copy(
            src_ref=src, dst_ref=dst, send_sem=send_sem.at[len(pending)], recv_sem=recv_sem.at[receive],
            device_id=device, device_id_type=MESH,
        )
        copy.start()
        pending.append(copy)

    def arrived(dst, receive):
        pltpu.make_async_remote_copy(
            src_ref=dst, dst_ref=dst, send_sem=send_sem.at[0], recv_sem=recv_sem.at[receive],
            device_id={"ch": sibling}, device_id_type=MESH,
        ).wait_recv()

    embed[...] = jnp.zeros_like(embed)
    loads = {}
    for name, src, dst in (
        ("tokens", tokens_in, tokens_ref),
        ("embedding", embedding_in, embed.at[pl.ds(0, 4)]),
        ("hidden", hidden_in, hidden_ref),
        ("cot", cot_in.at[pl.ds(0, half)], cot_near),
        ("order", order_in, order_ref),
        ("w_in", w_in_in, w_in_ref),
        ("w_gate", w_gate_in, w_gate_ref),
        ("w_out", w_out_in, w_out_ref),
        ("conv_w", conv_w_in, conv_w_ref),
        ("gain", gain_in, gain_ref),
    ):
        loads[name] = pltpu.make_async_copy(src, dst, local_sem.at[len(loads)])
        loads[name].start()
    stores = []

    def store_out(src, dst):
        copy = pltpu.make_async_copy(src, dst, local_sem.at[len(loads) + len(stores)])
        copy.start()
        stores.append(copy)

    for name in ("tokens", "embedding", "hidden"):
        loads[name].wait()
    hot = (lax.broadcasted_iota(jnp.int32, (16, rows), 0) == tokens_ref[...]).astype(F32).astype(BF16)
    looked_up = dot(hot, embed[...], (0, 0))
    block_in[ch] = (hidden_ref[...].astype(F32) + looked_up).astype(BF16)

    pl.semaphore_wait(barrier, len(greeted))

    parts = ((rows - FWD_LEFT, FWD_LEFT), (0, FWD_RIGHT), (FWD_RIGHT, rows - FWD_LEFT - FWD_RIGHT))
    gather = base("gather", 3 * groups)

    def gather_part(i, slot):
        return block_in.at[slot, pl.ds(parts[i][0], parts[i][1])]

    def gather_send(i, slot, target):
        send(gather_part(i, slot), gather_part(i, slot), gather + i * groups + slot, {"ch": target})

    def gather_wait(i, slot):
        arrived(gather_part(i, slot), gather + i * groups + slot)

    for i in range(3):
        gather_send(i, ch, across)
    send(block_in.at[ch], block_in.at[ch], gather + ch, {"ch": sibling})
    cot_sem = base("cot", 1)
    send(cot_in.at[pl.ds(half, half)], cot_far, cot_sem, {"seq": mirror})

    loads["order"].wait()
    for start in range(0, full, 128):
        place = lax.broadcasted_iota(jnp.int32, (128, full), 0) + start
        permute[start : start + 128, :] = (place == order_ref[...]).astype(F32).astype(BF16)
    flip = (
        lax.broadcasted_iota(jnp.int32, (2 * eighth, 2 * eighth), 0)
        + lax.broadcasted_iota(jnp.int32, (2 * eighth, 2 * eighth), 1)
        == 2 * eighth - 1
    ).astype(F32).astype(BF16)

    def terms(source, part):
        value = dot(source[...], w_out_ref[...], (1, 1)).astype(BF16)
        for q in range(groups):
            start = q * eighth if part == 0 else half - eighth - q * eighth
            span = slice(part * eighth, (part + 1) * eighth)
            term_send[q, span, :] = value[start : start + eighth]
            cot_mix[q, span, :] = source[start : start + eighth, :]

    loads["cot"].wait()
    loads["w_out"].wait()
    terms(cot_near, 0)

    def project(i, weights):
        start, size = parts[i]
        total = jnp.zeros((size, width), F32)
        for k in range(groups):
            total = total + dot(block_in[k, start : start + size, :], weights[k * width : (k + 1) * width, :], (1, 0))
        return total

    loads["w_in"].wait()
    halo = base("halo", 2)
    for i in range(2):
        gather_wait(i, across)
        gather_send(i, across, sibling)
    for i in range(2):
        start, size = parts[i]
        if i == 0:
            arrived(block_in.at[sibling], gather + sibling)
        gather_wait(i, diagonal)
        projected = project(i, w_in_ref).astype(BF16)
        level0[FWD_LEFT + start : FWD_LEFT + start + size, :] = projected.astype(F32)
        keep = pl.ds(0, FWD_LEFT) if i == 0 else pl.ds(FWD_LEFT, FWD_RIGHT)
        halo_send[keep, :] = projected
        send(halo_send.at[keep], halo_recv.at[keep], halo + i, {"seq": after if i == 0 else before})
    gather_wait(2, across)
    gather_send(2, across, sibling)
    loads["w_gate"].wait()
    for i in range(2):
        start, size = parts[i]
        gate_pre[start : start + size, :] = project(i, w_gate_ref)

    arrived(cot_far, cot_sem)
    terms(cot_far, 1)
    term = base("term", 3)
    gather_wait(2, diagonal)
    for i in range(2):
        target = i * 2 + 1 - core
        send(term_send.at[target], term_recv.at[i], term + i, {"ch": sibling})
    start, size = parts[2]
    level0[FWD_LEFT + start : FWD_LEFT + start + size, :] = project(2, w_in_ref).astype(BF16).astype(F32)
    gate_pre[start : start + size, :] = project(2, w_gate_ref)

    loads["conv_w"].wait()
    loads["gain"].wait()
    arrived(halo_recv.at[pl.ds(0, FWD_LEFT)], halo)
    arrived(halo_recv.at[pl.ds(FWD_LEFT, FWD_RIGHT)], halo + 1)
    own = FWD_LEFT + rows
    level0[0:FWD_LEFT, :] = halo_recv[0:FWD_LEFT, :].astype(F32) * left_live
    level0[own : own + FWD_RIGHT, :] = halo_recv[FWD_LEFT : FWD_LEFT + FWD_RIGHT, :].astype(F32) * right_live

    def convolve(source, level, sign, lo, hi, live, store):
        dilation = DILATIONS[level]
        for start, size in pieces(lo, hi):
            total = jnp.zeros((size, width), F32)
            for t in range(4):
                begin = start + sign * (t - 2) * dilation
                total = total + conv_w_ref[level, t : t + 1, :] * source[begin : begin + size, :]
            if live is not None:
                total = total * live
            store(start, size, total.astype(BF16).astype(F32))

    def into(target):
        def store(start, size, value):
            target[start : start + size, :] = value
        return store

    for level, (source, target) in enumerate(((level0, level1), (level1, level2))):
        lo, hi = ((8, own + 72), (24, own + 64))[level]
        convolve(source, level, 1, lo, FWD_LEFT, left_live, into(target))
        convolve(source, level, 1, FWD_LEFT, own, None, into(target))
        convolve(source, level, 1, own, hi, right_live, into(target))

    def store_gated(start, size, value):
        start = start - FWD_LEFT
        level3[start : start + size, :] = value
        gate = gate_pre[start : start + size, :]
        gated[start : start + size, :] = (value * (gate * jax.nn.sigmoid(gate))).astype(BF16)

    convolve(level2, 2, 1, FWD_LEFT, own, None, store_gated)

    mix = base("mix", 2 * groups)
    for q in range(groups):
        send(
            gated.at[pl.ds(rows - eighth - q * eighth, eighth)], both.at[ch, pl.ds(eighth, eighth)],
            mix + groups + ch, {"seq": mirror, "ch": q},
        )
    for d in range(1, groups):
        q = lax.rem(ch + d, groups)
        send(gated.at[top(q)], both.at[ch, pl.ds(0, eighth)], mix + ch, {"ch": q})
    both[ch, 0:eighth, :] = gated[top(ch), :]

    for i in range(2):
        arrived(term_recv.at[i], term + i)
    term_send[across] = (term_send[across].astype(F32) + term_recv[1 - x_lo].astype(F32)).astype(BF16)
    send(term_send.at[across], term_cross, term + 2, {"ch": across})
    arrived(term_cross, term + 2)
    grad_norm = term_send[ch].astype(F32) + term_recv[x_lo].astype(F32) + term_cross[...].astype(F32)
    scaled = grad_norm * gain_ref[...]

    for d in range(1, groups):
        q = lax.rem(ch + d, groups)
        arrived(both.at[q, pl.ds(0, eighth)], mix + q)
    for q in range(groups):
        arrived(both.at[q, pl.ds(eighth, eighth)], mix + groups + q)

    mine = jnp.concatenate([both[q] for q in range(groups)], axis=1)
    other = dot(flip, dot(mine, permute[...], (1, 0)).astype(BF16), (1, 0))
    combined = mine.astype(F32) + other
    inv_scale = lax.rsqrt(jnp.mean(combined * combined, axis=1, keepdims=True) + EPSILON)
    hat = combined * inv_scale
    normalized = (hat * gain_ref[...]).astype(BF16)
    norm_mix[ch] = normalized
    row_total = jnp.sum(scaled * hat, axis=1, keepdims=True)
    grad_comb = (inv_scale * (scaled - hat * (row_total * (1.0 / full)))).astype(BF16)
    turned = dot(flip, dot(grad_comb, permute[...], (1, 1)).astype(BF16), (1, 0))
    returned = (grad_comb.astype(F32) + turned).astype(BF16)
    for q in range(groups):
        grad_split[q] = returned[:, q * width : (q + 1) * width]
    back = base("back", 2 * groups)
    for q in range(groups):
        send(
            grad_split.at[q, pl.ds(eighth, eighth)], grad_gated.at[bottom(ch)],
            back + groups + ch, {"seq": mirror, "ch": q},
        )
    for d in range(1, groups):
        q = lax.rem(ch + d, groups)
        send(grad_split.at[q, pl.ds(0, eighth)], grad_gated.at[top(ch)], back + ch, {"ch": q})
    grad_gated[top(ch), :] = grad_split[ch, 0:eighth, :]

    norm = base("norm", groups)

    def norm_send(q, target):
        send(norm_mix.at[q], norm_mix.at[q], norm + q, {"ch": target})

    def norm_wait(q):
        arrived(norm_mix.at[q], norm + q)

    norm_send(ch, across)
    norm_send(ch, sibling)

    conv_rows = 16
    size = full // ring
    part = size // ring
    lanes = width // 2
    of_out, of_gate, late = 0, 1, 2
    finished = (grad_out_ref, grad_gate_ref, grad_in_ref)
    results = (grad_out_out, grad_gate_out, grad_in_out)

    def side(h):
        return slice(lanes * h, lanes * h + lanes)

    def span1(u):
        return pl.ds(0, size + (conv_rows if u == late else 0))

    def sem1(u, h, k):
        return base(("sum", u), 2 * ring) + h * ring + k

    def spread(u, value):
        for h in range(2):
            for k in range(ring):
                send1[u, h, k, 0:size, :] = value[k * size : (k + 1) * size, side(h)].astype(BF16)
        for d in range(1, ring):
            for h in range(2):
                t = lax.rem(me1[h] + d, ring)
                send(
                    send1.at[u, h, t, span1(u)], recv1.at[u, h, me1[h], span1(u)], sem1(u, h, me1[h]),
                    first_peer(h, t),
                )

    def span2(u, same):
        return pl.ds(u * part, part + (conv_rows if same and u == late else 0))

    def sem2(u, h, k):
        return base(("over", u), 2 * xs * ring) + h * xs * ring + k

    def second_sum(u):
        for h in range(2):
            total = send1[u, h, me1[h], 0:size, :].astype(F32)
            for d in range(1, ring):
                k = lax.rem(me1[h] + d, ring)
                arrived(recv1.at[u, h, k, span1(u)], sem1(u, h, k))
                total = total + recv1[u, h, k, 0:size, :].astype(F32)
            total = total.astype(BF16)
            for k in range(ring):
                send2[h, k, u * part : (u + 1) * part, :] = total[k * part : (k + 1) * part]
            if u == late:
                recv1[u, h, me1[h], size:, :] = send1[u, h, me1[h], size:, :]
                tail = jnp.zeros((conv_rows, lanes), F32)
                for k in range(ring):
                    tail = tail + recv1[u, h, k, size:, :].astype(F32)
                for k in range(ring):
                    send2[h, k, 3 * part :, :] = tail.astype(BF16)
            slot = my_x * ring + me2[h]
            for dx in reversed(range(xs)):
                for d in range(ring):
                    if dx or d:
                        x = lax.rem(my_x + dx, xs)
                        t = lax.rem(me2[h] + d, ring)
                        span = span2(u, dx == 0)
                        send(send2.at[h, t, span], recv2.at[h, slot, span], sem2(u, h, slot), second_peer(h, x, t))
            span = span2(u, True)
            recv2[h, slot, span, :] = send2[h, me2[h], span, :]

    def sem3(u, h, k):
        return base(("gather2", u), 2 * ring) + h * ring + k

    def sem4(u, h, k):
        return base(("gather1", u), 2 * ring) + h * ring + k

    conv_sem = base("conv", 2 * xs)

    def rows_of(k, m=None):
        if m is None:
            return pl.ds(pl.multiple_of(k * size, size), size)
        return pl.ds(pl.multiple_of(k * size + m * part, part), part)

    def done(u, h, k, m=None):
        return finished[u].at[rows_of(k, m), pl.ds(lanes * h, lanes)]

    def second_gather(u):
        for h in range(2):
            for dx in range(xs):
                for d in range(ring):
                    if dx or d:
                        k = lax.rem(my_x + dx, xs) * ring + lax.rem(me2[h] + d, ring)
                        arrived(recv2.at[h, k, span2(u, dx == 0)], sem2(u, h, k))
            total = jnp.zeros((part, lanes), F32)
            for k in range(xs * ring):
                total = total + recv2[h, k, span2(u, False), :].astype(F32)
            here = done(u, h, me1[h], me2[h])
            here[...] = total.astype(BF16)
            for d in range(1, ring):
                send(here, here, sem3(u, h, me2[h]), second_peer(h, my_x, lax.rem(me2[h] + d, ring)))
            if u == late:
                tail = jnp.zeros((conv_rows, lanes), F32)
                for t in range(ring):
                    tail = tail + recv2[h, my_x * ring + t, 3 * part :, :].astype(F32)
                conv_x[h, my_x] = tail.astype(BF16)
                for dx in range(1, xs):
                    here = conv_x.at[h, my_x]
                    send(here, here, conv_sem + h * xs + my_x, at(lax.rem(my_x + dx, xs), my_z, my_y))

    def first_gather(u):
        for h in range(2):
            for d in range(1, ring):
                k = lax.rem(me2[h] + d, ring)
                arrived(done(u, h, me1[h], k), sem3(u, h, k))
            here = done(u, h, me1[h])
            for d in range(1, ring):
                send(here, here, sem4(u, h, me1[h]), first_peer(h, lax.rem(me1[h] + d, ring)))

    def finish(u):
        for h in range(2):
            for d in range(1, ring):
                k = lax.rem(me1[h] + d, ring)
                arrived(done(u, h, k), sem4(u, h, k))
        store_out(finished[u], results[u])

    for d in range(1, groups):
        q = lax.rem(ch + d, groups)
        arrived(grad_gated.at[top(q)], back + q)
    for q in range(groups):
        arrived(grad_gated.at[bottom(q)], back + groups + q)
    own = BWD_LEFT + rows
    for start, tall in pieces(0, rows):
        gate = gate_pre[start : start + tall, :]
        sigmoid = jax.nn.sigmoid(gate)
        grad = grad_gated[start : start + tall, :].astype(F32)
        upstream = (grad * (gate * sigmoid)).astype(BF16)
        up3_low[start : start + tall, :] = upstream
        up3[BWD_LEFT + start : BWD_LEFT + start + tall, :] = upstream.astype(F32)
        gate_low[start : start + tall, :] = (
            grad * level3[start : start + tall, :] * sigmoid * (1.0 + gate * (1.0 - sigmoid))
        ).astype(BF16)
    halo_back = base("halo_back", 2)
    send(up3_low.at[pl.ds(0, BWD_RIGHT)], halo_late.at[pl.ds(BWD_LEFT, BWD_RIGHT)], halo_back, {"seq": before})
    send(
        up3_low.at[pl.ds(rows - BWD_LEFT, BWD_LEFT)], halo_late.at[pl.ds(0, BWD_LEFT)], halo_back + 1, {"seq": after}
    )

    def against_input(value):
        return jnp.concatenate([dot(block_in[k], value, (0, 0)) for k in range(groups)], axis=0)

    norm_wait(across)
    norm_send(across, sibling)
    spread(of_gate, against_input(gate_low[...]))
    norm_wait(sibling)
    norm_wait(diagonal)
    spread(of_out, dot(norm_mix[...].reshape(rows, full), cot_mix[...].reshape(rows, width), (0, 0)))

    arrived(halo_late.at[pl.ds(BWD_LEFT, BWD_RIGHT)], halo_back)
    arrived(halo_late.at[pl.ds(0, BWD_LEFT)], halo_back + 1)
    up3[0:BWD_LEFT, :] = halo_late[0:BWD_LEFT, :].astype(F32) * left_live
    up3[own : own + BWD_RIGHT, :] = halo_late[BWD_LEFT : BWD_LEFT + BWD_RIGHT, :].astype(F32) * right_live

    convolve(up3, 2, -1, 64, BWD_LEFT, left_live, into(up2))
    convolve(up3, 2, -1, BWD_LEFT, own, None, into(up2))
    convolve(up3, 2, -1, own, own + 24, right_live, into(up2))
    convolve(up2, 1, -1, 72, BWD_LEFT, left_live, into(up1))
    convolve(up2, 1, -1, BWD_LEFT, own, None, into(up1))
    convolve(up2, 1, -1, own, own + 8, right_live, into(up1))

    def store_last(start, tall, value):
        up0_low[start - BWD_LEFT : start - BWD_LEFT + tall, :] = value.astype(BF16)

    convolve(up1, 0, -1, BWD_LEFT, own, None, store_last)

    taps = []
    for level, (source, upstream) in enumerate(((level0, up1), (level1, up2), (level2, up3))):
        for t in range(4):
            total = jnp.zeros((8, width), F32)
            for start, tall in pieces(0, rows):
                begin = FWD_LEFT + start + (t - 2) * DILATIONS[level]
                term_product = (
                    upstream[BWD_LEFT + start : BWD_LEFT + start + tall, :] * source[begin : begin + tall, :]
                )
                total = total + jnp.sum(term_product.reshape(tall // 8, 8, width), axis=0)
            taps.append(jnp.sum(total, axis=0, keepdims=True))
    taps = jnp.concatenate(taps + [jnp.zeros((conv_rows - 12, width), F32)], axis=0).astype(BF16)
    for h in range(2):
        for k in range(ring):
            send1[late, h, k, size : size + conv_rows, :] = taps[:, side(h)]
    spread(late, against_input(up0_low[...]))

    second_sum(of_gate)

    product = dot(norm_mix[...].reshape(rows, full), w_out_ref[...], (1, 0))
    for q in range(groups):
        near = product[q * 2 * eighth : q * 2 * eighth + eighth]
        low = q * eighth
        output_ref[low : low + eighth, :] = (block_in[ch, low : low + eighth, :].astype(F32) + near).astype(BF16)
        low = half - eighth - q * eighth
        product_send[low : low + eighth, :] = product[q * 2 * eighth + eighth : (q + 1) * 2 * eighth].astype(BF16)
    product_sem = base("product", 1)
    send(product_send, product_recv, product_sem, {"seq": mirror})
    store_out(output_ref.at[pl.ds(0, half)], output_out.at[pl.ds(0, half)])

    second_sum(of_out)
    second_gather(of_gate)
    second_sum(late)
    second_gather(of_out)
    arrived(product_recv, product_sem)
    output_ref[half:rows, :] = (
        block_in[ch, half:rows, :].astype(F32) + product_recv[...].astype(F32)
    ).astype(BF16)
    store_out(output_ref.at[pl.ds(half, half)], output_out.at[pl.ds(half, half)])
    first_gather(of_gate)
    second_gather(late)
    first_gather(of_out)
    first_gather(late)
    for h in range(2):
        for dx in range(1, xs):
            x = lax.rem(my_x + dx, xs)
            arrived(conv_x.at[h, x], conv_sem + h * xs + x)
        tail = jnp.zeros((conv_rows, lanes), F32)
        for x in range(xs):
            tail = tail + conv_x[h, x].astype(F32)
        for level in range(3):
            grad_conv_ref[level, :, side(h)] = tail[4 * level : 4 * level + 4]
    store_out(grad_conv_ref, grad_conv_out)
    finish(of_gate)
    finish(of_out)
    for copy in pending:
        copy.wait_send()
    finish(late)
    for copy in stores:
        copy.wait()


def hand_over(*refs):
    count = len(refs) // 3
    given, results, stages, sems = refs[:count], refs[count : 2 * count], refs[2 * count : 3 * count], refs[-1]
    loads = [pltpu.make_async_copy(given[i], stages[i], sems.at[0, i]) for i in range(count)]
    stores = [pltpu.make_async_copy(stages[i], results[i], sems.at[1, i]) for i in range(count)]
    for copy in loads:
        copy.start()
    for load, store in zip(loads, stores):
        load.wait()
        store.start()
    for copy in stores:
        copy.wait()


def local(tokens, hidden, embedding, w_in, w_gate, conv_w, channel_order, gain, w_out, cotangent):
    rows, width = hidden.shape
    full = gain.shape[0]
    groups = lax.axis_size("ch")
    sizes = ring_sizes(lax.axis_size("seq"))
    xs, zs, ys = sizes
    size = full // ys
    part = size // zs
    eighth = rows // (2 * groups)
    extended = rows + FWD_LEFT + FWD_RIGHT
    anywhere = pl.BlockSpec(memory_space=pl.ANY)
    dma = pltpu.SemaphoreType.DMA

    def held(*shape, dtype=BF16):
        return pltpu.VMEM(shape, dtype)

    weight = jax.ShapeDtypeStruct((full, width), BF16)
    results = (
        jax.ShapeDtypeStruct((rows, width), BF16), weight, weight, weight, jax.ShapeDtypeStruct((3, 4, width), F32)
    )
    computed = pl.pallas_call(
        functools.partial(block_kernel, sizes, groups),
        out_shape=results,
        in_specs=[anywhere] * 10,
        out_specs=(anywhere,) * 5,
        scratch_shapes=[
            held(1, rows, dtype=jnp.int32),
            held(rows, width),
            held(full, width),
            held(full, width),
            held(3, 4, width, dtype=F32),
            held(1, full, dtype=jnp.int32),
            held(1, full, dtype=F32),
            held(full, width),
            held(rows, width),
            held(full, width),
            held(full, width),
            held(full, width),
            held(3, 4, width, dtype=F32),
            held(groups, rows, width),
            held(16, width),
            held(extended, width, dtype=F32),
            held(extended, width, dtype=F32),
            held(extended, width, dtype=F32),
            held(rows, width, dtype=F32),
            held(rows, width, dtype=F32),
            held(FWD_LEFT + FWD_RIGHT, width),
            held(FWD_LEFT + FWD_RIGHT, width),
            held(BWD_LEFT + BWD_RIGHT, width),
            held(rows, width),
            held(groups, 2 * eighth, width),
            held(full, full),
            held(rows // 2, width),
            held(rows // 2, width),
            held(groups, 2 * eighth, width),
            held(groups, 2 * eighth, full),
            held(2, 2 * eighth, full),
            held(2 * eighth, full),
            held(groups, 2 * eighth, full),
            held(groups, 2 * eighth, width),
            held(rows, width),
            held(extended, width, dtype=F32),
            held(extended, width, dtype=F32),
            held(extended, width, dtype=F32),
            held(rows // 2, width),
            held(rows // 2, width),
            held(rows, width),
            held(rows, width),
            held(rows, width),
            held(3, 2, ys, size + 16, width // 2),
            held(3, 2, ys, size + 16, width // 2),
            held(2, zs, 3 * part + 16, width // 2),
            held(2, xs * zs, 3 * part + 16, width // 2),
            held(2, xs, 16, width // 2),
            dma((SENDS,)),
            dma((RECEIVES,)),
            dma((32,)),
        ],
        compiler_params=pltpu.CompilerParams(
            collective_id=0, has_side_effects=True, vmem_limit_bytes=56 * 1024 * 1024
        ),
    )(
        tokens.reshape(1, rows), hidden, embedding, w_in, w_gate, conv_w, channel_order.reshape(1, full),
        gain.reshape(1, full), w_out, cotangent,
    )
    return pl.pallas_call(
        hand_over,
        out_shape=results,
        in_specs=[anywhere] * 5,
        out_specs=(anywhere,) * 5,
        scratch_shapes=[held(*result.shape, dtype=result.dtype) for result in results] + [dma((2, 5))],
        compiler_params=pltpu.CompilerParams(vmem_limit_bytes=60 * 1024 * 1024),
    )(*computed)


def solution(mesh):
    placed = (
        P("seq"),
        P("seq", "ch"),
        P(None, "ch"),
        P(None, "ch"),
        P(None, "ch"),
        P(None, None, "ch"),
        P(),
        P(),
        P(None, "ch"),
        P("seq", "ch"),
    )
    return jax.shard_map(
        local,
        mesh=mesh,
        in_specs=placed,
        out_specs=(
            P("seq", "ch"),
            P(None, "ch"),
            P(None, "ch"),
            P(None, "ch"),
            P(None, None, "ch"),
        ),
        check_vma=False,
    )
```

```python
import functools

import jax
import jax.numpy as jnp
from jax import lax
from jax.experimental import pallas as pl
from jax.experimental.pallas import tpu as pltpu
from jax.sharding import PartitionSpec as P

DILATIONS = (1, 8, 64)
EPSILON = 1e-06
MESH = pl.DeviceIdType.MESH
BF16 = jnp.bfloat16
F32 = jnp.float32

FWD_LEFT, FWD_RIGHT = 160, 80
BWD_LEFT, BWD_RIGHT = 80, 160
CHUNK = 64
SENDS = 272
RECEIVES = 304


def ring_sizes(count):
    return {128: (2, 8, 8), 8: (2, 2, 2), 4: (1, 2, 2)}[count]


def dot(a, b, contract):
    return lax.dot_general(a, b, ((contract[:1], contract[1:]), ((), ())), preferred_element_type=F32)


def pieces(lo, hi):
    return [(start, min(CHUNK, hi - start)) for start in range(lo, hi, CHUNK)]


def block_kernel(
    sizes, groups,
    tokens_in, hidden_in, embedding_in, w_in_in, w_gate_in, conv_w_in, order_in, gain_in, w_out_in, cot_in,
    output_out, grad_in_out, grad_gate_out, grad_out_out, grad_conv_out,
    tokens_ref, hidden_ref, w_in_ref, w_gate_ref, conv_w_ref, order_ref, gain_ref, w_out_ref,
    output_ref, grad_in_ref, grad_gate_ref, grad_out_ref, grad_conv_ref,
    block_in, embed, level0, level1, level2, level3, gate_pre, halo_send, halo_recv, halo_late,
    gated, both, permute, cot_near, cot_far, cot_mix, term_send, term_recv, term_cross, norm_mix, grad_split,
    grad_gated, up3, up2, up1, product_send, product_recv, up3_low, up0_low, gate_low,
    send1, recv1, send2, recv2, cross_x, send_sem, recv_sem, local_sem,
):
    xs, zs, ys = sizes
    count = xs * zs * ys
    rows, width = hidden_ref.shape
    full = width * groups
    eighth = rows // (2 * groups)
    half = rows // 2

    seq = lax.axis_index("seq")
    ch = lax.axis_index("ch")
    core = lax.rem(ch, 2)
    x_lo = lax.div(ch, 2)
    sibling = x_lo * 2 + 1 - core
    across = (1 - x_lo) * 2 + core
    diagonal = (1 - x_lo) * 2 + 1 - core
    mirror = count - 1 - seq
    after = lax.rem(seq + 1, count)
    before = lax.rem(seq + count - 1, count)
    my_y = lax.rem(seq, ys)
    my_z = lax.rem(lax.div(seq, ys), zs)
    my_x = lax.div(seq, ys * zs)
    left_live = (seq > 0).astype(F32)
    right_live = (seq < count - 1).astype(F32)

    def at(x, z, y):
        return {"seq": (x * zs + z) * ys + y}

    assert ys == zs
    ring = ys
    me1 = (my_y, my_z)
    me2 = (my_z, my_y)

    def first_peer(h, t):
        return at(my_x, my_z, t) if h == 0 else at(my_x, t, my_y)

    def second_peer(h, x, t):
        return at(x, t, my_y) if h == 0 else at(x, my_z, t)

    def top(q):
        return pl.ds(pl.multiple_of(q * eighth, eighth), eighth)

    def bottom(q):
        return pl.ds(pl.multiple_of(rows - eighth - q * eighth, eighth), eighth)

    barrier = pltpu.get_barrier_semaphore()
    greeted = []

    def greet(device):
        pl.semaphore_signal(barrier, inc=1, device_id=device, device_id_type=MESH)
        greeted.append(0)

    greet({"ch": sibling})
    greet({"ch": across})
    greet({"ch": diagonal})
    for q in range(groups):
        greet({"seq": mirror, "ch": q})
    greet({"seq": after})
    greet({"seq": before})
    for h in range(2):
        for d in range(1, ring):
            greet(first_peer(h, lax.rem(me1[h] + d, ring)))
    for dx in range(1, xs):
        x = lax.rem(my_x + dx, xs)
        for d in range(ring):
            greet(second_peer(0, x, lax.rem(my_z + d, ring)))
        for d in range(1, ring):
            greet(second_peer(1, x, lax.rem(my_y + d, ring)))

    pending = []
    bases = {}

    def base(name, size):
        if name not in bases:
            bases[name] = sum(taken for _, taken in bases.values()), size
        return bases[name][0]

    def send(src, dst, receive, device):
        copy = pltpu.make_async_remote_copy(
            src_ref=src, dst_ref=dst, send_sem=send_sem.at[len(pending)], recv_sem=recv_sem.at[receive],
            device_id=device, device_id_type=MESH,
        )
        copy.start()
        pending.append(copy)

    def arrived(dst, receive):
        pltpu.make_async_remote_copy(
            src_ref=dst, dst_ref=dst, send_sem=send_sem.at[0], recv_sem=recv_sem.at[receive],
            device_id={"ch": sibling}, device_id_type=MESH,
        ).wait_recv()

    embed[...] = jnp.zeros_like(embed)
    loads = {}
    for name, src, dst in (
        ("tokens", tokens_in, tokens_ref),
        ("embedding", embedding_in, embed.at[pl.ds(0, 4)]),
        ("hidden", hidden_in, hidden_ref),
        ("cot", cot_in.at[pl.ds(0, half)], cot_near),
        ("order", order_in, order_ref),
        ("w_in", w_in_in, w_in_ref),
        ("w_gate", w_gate_in, w_gate_ref),
        ("w_out", w_out_in, w_out_ref),
        ("conv_w", conv_w_in, conv_w_ref),
        ("gain", gain_in, gain_ref),
    ):
        loads[name] = pltpu.make_async_copy(src, dst, local_sem.at[len(loads)])
        loads[name].start()
    stores = []

    def store_out(src, dst):
        copy = pltpu.make_async_copy(src, dst, local_sem.at[len(loads) + len(stores)])
        copy.start()
        stores.append(copy)

    for name in ("tokens", "embedding", "hidden"):
        loads[name].wait()
    hot = (lax.broadcasted_iota(jnp.int32, (16, rows), 0) == tokens_ref[...]).astype(F32).astype(BF16)
    looked_up = dot(hot, embed[...], (0, 0))
    block_in[ch] = (hidden_ref[...].astype(F32) + looked_up).astype(BF16)

    pl.semaphore_wait(barrier, len(greeted))

    parts = ((rows - FWD_LEFT, FWD_LEFT), (0, FWD_RIGHT), (FWD_RIGHT, rows - FWD_LEFT - FWD_RIGHT))
    gather = base("gather", 3 * groups)

    def gather_part(i, slot):
        return block_in.at[slot, pl.ds(parts[i][0], parts[i][1])]

    def gather_send(i, slot, target):
        send(gather_part(i, slot), gather_part(i, slot), gather + i * groups + slot, {"ch": target})

    def gather_wait(i, slot):
        arrived(gather_part(i, slot), gather + i * groups + slot)

    for i in range(3):
        gather_send(i, ch, across)
    send(block_in.at[ch], block_in.at[ch], gather + ch, {"ch": sibling})
    cot_sem = base("cot", 1)
    send(cot_in.at[pl.ds(half, half)], cot_far, cot_sem, {"seq": mirror})

    loads["order"].wait()
    for start in range(0, full, 128):
        place = lax.broadcasted_iota(jnp.int32, (128, full), 0) + start
        permute[start : start + 128, :] = (place == order_ref[...]).astype(F32).astype(BF16)
    flip = (
        lax.broadcasted_iota(jnp.int32, (2 * eighth, 2 * eighth), 0)
        + lax.broadcasted_iota(jnp.int32, (2 * eighth, 2 * eighth), 1)
        == 2 * eighth - 1
    ).astype(F32).astype(BF16)

    def terms(source, part):
        value = dot(source[...], w_out_ref[...], (1, 1)).astype(BF16)
        for q in range(groups):
            start = q * eighth if part == 0 else half - eighth - q * eighth
            span = slice(part * eighth, (part + 1) * eighth)
            term_send[q, span, :] = value[start : start + eighth]
            cot_mix[q, span, :] = source[start : start + eighth, :]

    loads["cot"].wait()
    loads["w_out"].wait()
    terms(cot_near, 0)

    def project(i, weights):
        start, size = parts[i]
        total = jnp.zeros((size, width), F32)
        for k in range(groups):
            total = total + dot(block_in[k, start : start + size, :], weights[k * width : (k + 1) * width, :], (1, 0))
        return total

    loads["w_in"].wait()
    halo = base("halo", 2)
    for i in range(2):
        gather_wait(i, across)
        gather_send(i, across, sibling)
    for i in range(2):
        start, size = parts[i]
        if i == 0:
            arrived(block_in.at[sibling], gather + sibling)
        gather_wait(i, diagonal)
        projected = project(i, w_in_ref).astype(BF16)
        level0[FWD_LEFT + start : FWD_LEFT + start + size, :] = projected.astype(F32)
        keep = pl.ds(0, FWD_LEFT) if i == 0 else pl.ds(FWD_LEFT, FWD_RIGHT)
        halo_send[keep, :] = projected
        send(halo_send.at[keep], halo_recv.at[keep], halo + i, {"seq": after if i == 0 else before})
    gather_wait(2, across)
    gather_send(2, across, sibling)
    loads["w_gate"].wait()
    for i in range(2):
        start, size = parts[i]
        gate_pre[start : start + size, :] = project(i, w_gate_ref)

    arrived(cot_far, cot_sem)
    terms(cot_far, 1)
    term = base("term", 3)
    gather_wait(2, diagonal)
    for i in range(2):
        target = i * 2 + 1 - core
        send(term_send.at[target], term_recv.at[i], term + i, {"ch": sibling})
    start, size = parts[2]
    level0[FWD_LEFT + start : FWD_LEFT + start + size, :] = project(2, w_in_ref).astype(BF16).astype(F32)
    gate_pre[start : start + size, :] = project(2, w_gate_ref)

    loads["conv_w"].wait()
    loads["gain"].wait()
    arrived(halo_recv.at[pl.ds(0, FWD_LEFT)], halo)
    arrived(halo_recv.at[pl.ds(FWD_LEFT, FWD_RIGHT)], halo + 1)
    own = FWD_LEFT + rows
    level0[0:FWD_LEFT, :] = halo_recv[0:FWD_LEFT, :].astype(F32) * left_live
    level0[own : own + FWD_RIGHT, :] = halo_recv[FWD_LEFT : FWD_LEFT + FWD_RIGHT, :].astype(F32) * right_live

    def convolve(source, level, sign, lo, hi, live, store):
        dilation = DILATIONS[level]
        for start, size in pieces(lo, hi):
            total = jnp.zeros((size, width), F32)
            for t in range(4):
                begin = start + sign * (t - 2) * dilation
                total = total + conv_w_ref[level, t : t + 1, :] * source[begin : begin + size, :]
            if live is not None:
                total = total * live
            store(start, size, total.astype(BF16).astype(F32))

    def into(target):
        def store(start, size, value):
            target[start : start + size, :] = value
        return store

    for level, (source, target) in enumerate(((level0, level1), (level1, level2))):
        lo, hi = ((8, own + 72), (24, own + 64))[level]
        convolve(source, level, 1, lo, FWD_LEFT, left_live, into(target))
        convolve(source, level, 1, FWD_LEFT, own, None, into(target))
        convolve(source, level, 1, own, hi, right_live, into(target))

    def store_gated(start, size, value):
        start = start - FWD_LEFT
        level3[start : start + size, :] = value
        gate = gate_pre[start : start + size, :]
        gated[start : start + size, :] = (value * (gate * jax.nn.sigmoid(gate))).astype(BF16)

    convolve(level2, 2, 1, FWD_LEFT, own, None, store_gated)

    mix = base("mix", 2 * groups)
    for q in range(groups):
        send(
            gated.at[pl.ds(rows - eighth - q * eighth, eighth)], both.at[ch, pl.ds(eighth, eighth)],
            mix + groups + ch, {"seq": mirror, "ch": q},
        )
    for d in range(1, groups):
        q = lax.rem(ch + d, groups)
        send(gated.at[top(q)], both.at[ch, pl.ds(0, eighth)], mix + ch, {"ch": q})
    both[ch, 0:eighth, :] = gated[top(ch), :]

    for i in range(2):
        arrived(term_recv.at[i], term + i)
    term_send[across] = (term_send[across].astype(F32) + term_recv[1 - x_lo].astype(F32)).astype(BF16)
    send(term_send.at[across], term_cross, term + 2, {"ch": across})
    arrived(term_cross, term + 2)
    grad_norm = term_send[ch].astype(F32) + term_recv[x_lo].astype(F32) + term_cross[...].astype(F32)
    scaled = grad_norm * gain_ref[...]

    for d in range(1, groups):
        q = lax.rem(ch + d, groups)
        arrived(both.at[q, pl.ds(0, eighth)], mix + q)
    for q in range(groups):
        arrived(both.at[q, pl.ds(eighth, eighth)], mix + groups + q)

    mine = jnp.concatenate([both[q] for q in range(groups)], axis=1)
    other = dot(flip, dot(mine, permute[...], (1, 0)).astype(BF16), (1, 0))
    combined = mine.astype(F32) + other
    inv_scale = lax.rsqrt(jnp.mean(combined * combined, axis=1, keepdims=True) + EPSILON)
    hat = combined * inv_scale
    normalized = (hat * gain_ref[...]).astype(BF16)
    norm_mix[ch] = normalized
    row_total = jnp.sum(scaled * hat, axis=1, keepdims=True)
    grad_comb = (inv_scale * (scaled - hat * (row_total * (1.0 / full)))).astype(BF16)
    turned = dot(flip, dot(grad_comb, permute[...], (1, 1)).astype(BF16), (1, 0))
    returned = (grad_comb.astype(F32) + turned).astype(BF16)
    for q in range(groups):
        grad_split[q] = returned[:, q * width : (q + 1) * width]
    back = base("back", 2 * groups)
    for q in range(groups):
        send(
            grad_split.at[q, pl.ds(eighth, eighth)], grad_gated.at[bottom(ch)],
            back + groups + ch, {"seq": mirror, "ch": q},
        )
    for d in range(1, groups):
        q = lax.rem(ch + d, groups)
        send(grad_split.at[q, pl.ds(0, eighth)], grad_gated.at[top(ch)], back + ch, {"ch": q})
    grad_gated[top(ch), :] = grad_split[ch, 0:eighth, :]

    norm = base("norm", groups)

    def norm_send(q, target):
        send(norm_mix.at[q], norm_mix.at[q], norm + q, {"ch": target})

    def norm_wait(q):
        arrived(norm_mix.at[q], norm + q)

    norm_send(ch, across)
    norm_send(ch, sibling)

    conv_rows = 16
    size = full // ring
    part = size // ring
    lanes = width // 2
    of_out, of_gate, late = 0, 1, 2
    finished = (grad_out_ref, grad_gate_ref, grad_in_ref)
    results = (grad_out_out, grad_gate_out, grad_in_out)

    def side(h):
        return slice(lanes * h, lanes * h + lanes)

    def span1(u):
        return pl.ds(0, size + (conv_rows if u == late else 0))

    def sem1(u, h, k):
        return base(("sum", u), 2 * ring) + h * ring + k

    def spread(u, value):
        for h in range(2):
            for k in range(ring):
                send1[u, h, k, 0:size, :] = value[k * size : (k + 1) * size, side(h)].astype(BF16)
        for d in range(1, ring):
            for h in range(2):
                t = lax.rem(me1[h] + d, ring)
                send(
                    send1.at[u, h, t, span1(u)], recv1.at[u, h, me1[h], span1(u)], sem1(u, h, me1[h]),
                    first_peer(h, t),
                )

    def span2(u):
        return pl.ds(u * part, part + (conv_rows if u == late else 0))

    def sem2(u, h, k):
        return base(("over", u), 2 * ring) + h * ring + k

    def second_sum(u):
        for h in range(2):
            total = send1[u, h, me1[h], 0:size, :].astype(F32)
            for d in range(1, ring):
                k = lax.rem(me1[h] + d, ring)
                arrived(recv1.at[u, h, k, span1(u)], sem1(u, h, k))
                total = total + recv1[u, h, k, 0:size, :].astype(F32)
            total = total.astype(BF16)
            for k in range(ring):
                send2[h, k, u * part : (u + 1) * part, :] = total[k * part : (k + 1) * part]
            if u == late:
                recv1[u, h, me1[h], size:, :] = send1[u, h, me1[h], size:, :]
                tail = jnp.zeros((conv_rows, lanes), F32)
                for k in range(ring):
                    tail = tail + recv1[u, h, k, size:, :].astype(F32)
                for k in range(ring):
                    send2[h, k, 3 * part :, :] = tail.astype(BF16)
            span = span2(u)
            for d in range(1, ring):
                t = lax.rem(me2[h] + d, ring)
                send(send2.at[h, t, span], recv2.at[h, me2[h], span], sem2(u, h, me2[h]), second_peer(h, my_x, t))
            recv2[h, me2[h], span, :] = send2[h, me2[h], span, :]

    def sem_x(u, h, x):
        return base(("cross", u), 2 * xs) + h * xs + x

    def cross(u):
        span = span2(u)
        for h in range(2):
            for d in range(1, ring):
                k = lax.rem(me2[h] + d, ring)
                arrived(recv2.at[h, k, span], sem2(u, h, k))
            total = recv2[h, 0, span, :].astype(F32)
            for k in range(1, ring):
                total = total + recv2[h, k, span, :].astype(F32)
            here = cross_x.at[h, my_x, span]
            here[...] = total.astype(BF16)
            for dx in range(1, xs):
                send(here, here, sem_x(u, h, my_x), at(lax.rem(my_x + dx, xs), my_z, my_y))

    def sem3(u, h, k):
        return base(("gather2", u), 2 * ring) + h * ring + k

    def sem4(u, h, k):
        return base(("gather1", u), 2 * ring) + h * ring + k

    def rows_of(k, m=None):
        if m is None:
            return pl.ds(pl.multiple_of(k * size, size), size)
        return pl.ds(pl.multiple_of(k * size + m * part, part), part)

    def done(u, h, k, m=None):
        return finished[u].at[rows_of(k, m), pl.ds(lanes * h, lanes)]

    def second_gather(u):
        span = span2(u)
        for h in range(2):
            for dx in range(1, xs):
                x = lax.rem(my_x + dx, xs)
                arrived(cross_x.at[h, x, span], sem_x(u, h, x))
            total = cross_x[h, 0, span, :].astype(F32)
            for x in range(1, xs):
                total = total + cross_x[h, x, span, :].astype(F32)
            here = done(u, h, me1[h], me2[h])
            here[...] = total[0:part].astype(BF16)
            for d in range(1, ring):
                send(here, here, sem3(u, h, me2[h]), second_peer(h, my_x, lax.rem(me2[h] + d, ring)))
            if u == late:
                for level in range(3):
                    low = part + 4 * level
                    grad_conv_ref[level, :, side(h)] = total[low : low + 4]

    def first_gather(u):
        for h in range(2):
            for d in range(1, ring):
                k = lax.rem(me2[h] + d, ring)
                arrived(done(u, h, me1[h], k), sem3(u, h, k))
            here = done(u, h, me1[h])
            for d in range(1, ring):
                if u == late or d != ring // 2:
                    send(here, here, sem4(u, h, me1[h]), first_peer(h, lax.rem(me1[h] + d, ring)))

    def relay(u):
        for h in range(2):
            k = lax.rem(me1[h] + ring // 2 - 1, ring)
            here = done(u, h, k)
            if ring > 2:
                arrived(here, sem4(u, h, k))
            send(here, here, sem4(u, h, k), first_peer(h, lax.rem(me1[h] + ring - 1, ring)))

    def finish(u):
        for h in range(2):
            for d in range(1, ring):
                k = lax.rem(me1[h] + d, ring)
                if u == late or ring == 2 or d != ring // 2 - 1:
                    arrived(done(u, h, k), sem4(u, h, k))
                if u == late and h == 1:
                    store_out(finished[u].at[rows_of(k)], results[u].at[rows_of(k)])
        if u == late:
            store_out(finished[u].at[rows_of(me1[1])], results[u].at[rows_of(me1[1])])
        else:
            store_out(finished[u], results[u])

    for d in range(1, groups):
        q = lax.rem(ch + d, groups)
        arrived(grad_gated.at[top(q)], back + q)
    for q in range(groups):
        arrived(grad_gated.at[bottom(q)], back + groups + q)
    own = BWD_LEFT + rows
    for start, tall in pieces(0, rows):
        gate = gate_pre[start : start + tall, :]
        sigmoid = jax.nn.sigmoid(gate)
        grad = grad_gated[start : start + tall, :].astype(F32)
        upstream = (grad * (gate * sigmoid)).astype(BF16)
        up3_low[start : start + tall, :] = upstream
        up3[BWD_LEFT + start : BWD_LEFT + start + tall, :] = upstream.astype(F32)
        gate_low[start : start + tall, :] = (
            grad * level3[start : start + tall, :] * sigmoid * (1.0 + gate * (1.0 - sigmoid))
        ).astype(BF16)
    halo_back = base("halo_back", 2)
    send(up3_low.at[pl.ds(0, BWD_RIGHT)], halo_late.at[pl.ds(BWD_LEFT, BWD_RIGHT)], halo_back, {"seq": before})
    send(
        up3_low.at[pl.ds(rows - BWD_LEFT, BWD_LEFT)], halo_late.at[pl.ds(0, BWD_LEFT)], halo_back + 1, {"seq": after}
    )

    def against_input(value):
        return jnp.concatenate([dot(block_in[k], value, (0, 0)) for k in range(groups)], axis=0)

    norm_wait(across)
    norm_send(across, sibling)
    spread(of_gate, against_input(gate_low[...]))
    norm_wait(sibling)
    norm_wait(diagonal)
    spread(of_out, dot(norm_mix[...].reshape(rows, full), cot_mix[...].reshape(rows, width), (0, 0)))

    arrived(halo_late.at[pl.ds(BWD_LEFT, BWD_RIGHT)], halo_back)
    arrived(halo_late.at[pl.ds(0, BWD_LEFT)], halo_back + 1)
    up3[0:BWD_LEFT, :] = halo_late[0:BWD_LEFT, :].astype(F32) * left_live
    up3[own : own + BWD_RIGHT, :] = halo_late[BWD_LEFT : BWD_LEFT + BWD_RIGHT, :].astype(F32) * right_live

    convolve(up3, 2, -1, 64, BWD_LEFT, left_live, into(up2))
    convolve(up3, 2, -1, BWD_LEFT, own, None, into(up2))
    convolve(up3, 2, -1, own, own + 24, right_live, into(up2))
    convolve(up2, 1, -1, 72, BWD_LEFT, left_live, into(up1))
    convolve(up2, 1, -1, BWD_LEFT, own, None, into(up1))
    convolve(up2, 1, -1, own, own + 8, right_live, into(up1))

    def store_last(start, tall, value):
        up0_low[start - BWD_LEFT : start - BWD_LEFT + tall, :] = value.astype(BF16)

    convolve(up1, 0, -1, BWD_LEFT, own, None, store_last)

    taps = []
    for level, (source, upstream) in enumerate(((level0, up1), (level1, up2), (level2, up3))):
        for t in range(4):
            total = jnp.zeros((8, width), F32)
            for start, tall in pieces(0, rows):
                begin = FWD_LEFT + start + (t - 2) * DILATIONS[level]
                term_product = (
                    upstream[BWD_LEFT + start : BWD_LEFT + start + tall, :] * source[begin : begin + tall, :]
                )
                total = total + jnp.sum(term_product.reshape(tall // 8, 8, width), axis=0)
            taps.append(jnp.sum(total, axis=0, keepdims=True))
    taps = jnp.concatenate(taps + [jnp.zeros((conv_rows - 12, width), F32)], axis=0).astype(BF16)
    for h in range(2):
        for k in range(ring):
            send1[late, h, k, size : size + conv_rows, :] = taps[:, side(h)]
    spread(late, against_input(up0_low[...]))

    second_sum(of_gate)

    product = dot(norm_mix[...].reshape(rows, full), w_out_ref[...], (1, 0))
    for q in range(groups):
        near = product[q * 2 * eighth : q * 2 * eighth + eighth]
        low = q * eighth
        output_ref[low : low + eighth, :] = (block_in[ch, low : low + eighth, :].astype(F32) + near).astype(BF16)
        low = half - eighth - q * eighth
        product_send[low : low + eighth, :] = product[q * 2 * eighth + eighth : (q + 1) * 2 * eighth].astype(BF16)
    product_sem = base("product", 1)
    send(product_send, product_recv, product_sem, {"seq": mirror})
    store_out(output_ref.at[pl.ds(0, half)], output_out.at[pl.ds(0, half)])

    second_sum(of_out)
    cross(of_gate)
    second_sum(late)
    second_gather(of_gate)
    cross(of_out)
    arrived(product_recv, product_sem)
    output_ref[half:rows, :] = (
        block_in[ch, half:rows, :].astype(F32) + product_recv[...].astype(F32)
    ).astype(BF16)
    store_out(output_ref.at[pl.ds(half, half)], output_out.at[pl.ds(half, half)])
    cross(late)
    second_gather(of_out)
    first_gather(of_gate)
    second_gather(late)
    first_gather(of_out)
    first_gather(late)
    relay(of_gate)
    relay(of_out)
    store_out(grad_conv_ref, grad_conv_out)
    finish(of_gate)
    finish(of_out)
    for copy in pending:
        copy.wait_send()
    finish(late)
    for copy in stores:
        copy.wait()


def hand_over(*refs):
    count = len(refs) // 3
    given, results, stages, sems = refs[:count], refs[count : 2 * count], refs[2 * count : 3 * count], refs[-1]
    loads = [pltpu.make_async_copy(given[i], stages[i], sems.at[0, i]) for i in range(count)]
    stores = [pltpu.make_async_copy(stages[i], results[i], sems.at[1, i]) for i in range(count)]
    for copy in loads:
        copy.start()
    for load, store in zip(loads, stores):
        load.wait()
        store.start()
    for copy in stores:
        copy.wait()


def local(tokens, hidden, embedding, w_in, w_gate, conv_w, channel_order, gain, w_out, cotangent):
    rows, width = hidden.shape
    full = gain.shape[0]
    groups = lax.axis_size("ch")
    sizes = ring_sizes(lax.axis_size("seq"))
    xs, zs, ys = sizes
    size = full // ys
    part = size // zs
    eighth = rows // (2 * groups)
    extended = rows + FWD_LEFT + FWD_RIGHT
    anywhere = pl.BlockSpec(memory_space=pl.ANY)
    dma = pltpu.SemaphoreType.DMA

    def held(*shape, dtype=BF16):
        return pltpu.VMEM(shape, dtype)

    weight = jax.ShapeDtypeStruct((full, width), BF16)
    results = (
        jax.ShapeDtypeStruct((rows, width), BF16), weight, weight, weight, jax.ShapeDtypeStruct((3, 4, width), F32)
    )
    computed = pl.pallas_call(
        functools.partial(block_kernel, sizes, groups),
        out_shape=results,
        in_specs=[anywhere] * 10,
        out_specs=(anywhere,) * 5,
        scratch_shapes=[
            held(1, rows, dtype=jnp.int32),
            held(rows, width),
            held(full, width),
            held(full, width),
            held(3, 4, width, dtype=F32),
            held(1, full, dtype=jnp.int32),
            held(1, full, dtype=F32),
            held(full, width),
            held(rows, width),
            held(full, width),
            held(full, width),
            held(full, width),
            held(3, 4, width, dtype=F32),
            held(groups, rows, width),
            held(16, width),
            held(extended, width, dtype=F32),
            held(extended, width, dtype=F32),
            held(extended, width, dtype=F32),
            held(rows, width, dtype=F32),
            held(rows, width, dtype=F32),
            held(FWD_LEFT + FWD_RIGHT, width),
            held(FWD_LEFT + FWD_RIGHT, width),
            held(BWD_LEFT + BWD_RIGHT, width),
            held(rows, width),
            held(groups, 2 * eighth, width),
            held(full, full),
            held(rows // 2, width),
            held(rows // 2, width),
            held(groups, 2 * eighth, width),
            held(groups, 2 * eighth, full),
            held(2, 2 * eighth, full),
            held(2 * eighth, full),
            held(groups, 2 * eighth, full),
            held(groups, 2 * eighth, width),
            held(rows, width),
            held(extended, width, dtype=F32),
            held(extended, width, dtype=F32),
            held(extended, width, dtype=F32),
            held(rows // 2, width),
            held(rows // 2, width),
            held(rows, width),
            held(rows, width),
            held(rows, width),
            held(3, 2, ys, size + 16, width // 2),
            held(3, 2, ys, size + 16, width // 2),
            held(2, zs, 3 * part + 16, width // 2),
            held(2, zs, 3 * part + 16, width // 2),
            held(2, xs, 3 * part + 16, width // 2),
            dma((SENDS,)),
            dma((RECEIVES,)),
            dma((32,)),
        ],
        compiler_params=pltpu.CompilerParams(
            collective_id=0, has_side_effects=True, vmem_limit_bytes=56 * 1024 * 1024
        ),
    )(
        tokens.reshape(1, rows), hidden, embedding, w_in, w_gate, conv_w, channel_order.reshape(1, full),
        gain.reshape(1, full), w_out, cotangent,
    )
    return pl.pallas_call(
        hand_over,
        out_shape=results,
        in_specs=[anywhere] * 5,
        out_specs=(anywhere,) * 5,
        scratch_shapes=[held(*result.shape, dtype=result.dtype) for result in results] + [dma((2, 5))],
        compiler_params=pltpu.CompilerParams(vmem_limit_bytes=60 * 1024 * 1024),
    )(*computed)


def solution(mesh):
    placed = (
        P("seq"),
        P("seq", "ch"),
        P(None, "ch"),
        P(None, "ch"),
        P(None, "ch"),
        P(None, None, "ch"),
        P(),
        P(),
        P(None, "ch"),
        P("seq", "ch"),
    )
    return jax.shard_map(
        local,
        mesh=mesh,
        in_specs=placed,
        out_specs=(
            P("seq", "ch"),
            P(None, "ch"),
            P(None, "ch"),
            P(None, "ch"),
            P(None, None, "ch"),
        ),
        check_vma=False,
    )
```

```python
import functools

import jax
import jax.numpy as jnp
from jax import lax
from jax.experimental import pallas as pl
from jax.experimental.pallas import tpu as pltpu
from jax.sharding import PartitionSpec as P

DILATIONS = (1, 8, 64)
EPSILON = 1e-06
MESH = pl.DeviceIdType.MESH
BF16 = jnp.bfloat16
F32 = jnp.float32

FWD_LEFT, FWD_RIGHT = 160, 80
BWD_LEFT, BWD_RIGHT = 80, 160
CHUNK = 64
SENDS = 272
RECEIVES = 304


def ring_sizes(count):
    return {128: (2, 8, 8), 16: (1, 4, 4), 8: (2, 2, 2), 4: (1, 2, 2)}[count]


def dot(a, b, contract):
    return lax.dot_general(a, b, ((contract[:1], contract[1:]), ((), ())), preferred_element_type=F32)


def pieces(lo, hi):
    return [(start, min(CHUNK, hi - start)) for start in range(lo, hi, CHUNK)]


def block_kernel(
    sizes, groups,
    tokens_in, hidden_in, embedding_in, w_in_in, w_gate_in, conv_w_in, order_in, gain_in, w_out_in, cot_in,
    output_out, grad_in_out, grad_gate_out, grad_out_out, grad_conv_out,
    tokens_ref, hidden_ref, embedding_ref, w_in_ref, w_gate_ref, conv_w_ref, order_ref, gain_ref, w_out_ref,
    output_ref, grad_in_ref, grad_gate_ref, grad_out_ref, grad_conv_ref,
    block_in, embed, level0, level1, level2, level3, gate_pre, halo_send, halo_recv, halo_late,
    gated, both, permute, cot_near, cot_far, cot_mix, term_send, term_recv, term_cross, norm_mix, grad_split,
    grad_gated, up3, up2, up1, product_send, product_recv, up3_low, up0_low, gate_low,
    send1, recv1, send2, recv2, cross_x, send_sem, recv_sem, local_sem,
):
    xs, zs, ys = sizes
    count = xs * zs * ys
    rows, width = hidden_ref.shape
    full = width * groups
    eighth = rows // (2 * groups)
    half = rows // 2

    seq = lax.axis_index("seq")
    ch = lax.axis_index("ch")
    core = lax.rem(ch, 2)
    x_lo = lax.div(ch, 2)
    sibling = x_lo * 2 + 1 - core
    across = (1 - x_lo) * 2 + core
    diagonal = (1 - x_lo) * 2 + 1 - core
    mirror = count - 1 - seq
    after = lax.rem(seq + 1, count)
    before = lax.rem(seq + count - 1, count)
    my_y = lax.rem(seq, ys)
    my_z = lax.rem(lax.div(seq, ys), zs)
    my_x = lax.div(seq, ys * zs)
    left_live = (seq > 0).astype(F32)
    right_live = (seq < count - 1).astype(F32)

    def at(x, z, y):
        return {"seq": (x * zs + z) * ys + y}

    assert ys == zs
    ring = ys
    me1 = (my_y, my_z)
    me2 = (my_z, my_y)

    def first_peer(h, t):
        return at(my_x, my_z, t) if h == 0 else at(my_x, t, my_y)

    def second_peer(h, x, t):
        return at(x, t, my_y) if h == 0 else at(x, my_z, t)

    def top(q):
        return pl.ds(pl.multiple_of(q * eighth, eighth), eighth)

    def bottom(q):
        return pl.ds(pl.multiple_of(rows - eighth - q * eighth, eighth), eighth)

    barrier = pltpu.get_barrier_semaphore()
    greeted = []

    def greet(device):
        pl.semaphore_signal(barrier, inc=1, device_id=device, device_id_type=MESH)
        greeted.append(0)

    greet({"ch": sibling})
    greet({"ch": across})
    greet({"ch": diagonal})
    for q in range(groups):
        greet({"seq": mirror, "ch": q})
    greet({"seq": after})
    greet({"seq": before})
    for h in range(2):
        for d in range(1, ring):
            greet(first_peer(h, lax.rem(me1[h] + d, ring)))
    for dx in range(1, xs):
        x = lax.rem(my_x + dx, xs)
        for d in range(ring):
            greet(second_peer(0, x, lax.rem(my_z + d, ring)))
        for d in range(1, ring):
            greet(second_peer(1, x, lax.rem(my_y + d, ring)))

    pending = []
    bases = {}

    def base(name, size):
        if name not in bases:
            bases[name] = sum(taken for _, taken in bases.values()), size
        return bases[name][0]

    def send(src, dst, receive, device):
        copy = pltpu.make_async_remote_copy(
            src_ref=src, dst_ref=dst, send_sem=send_sem.at[len(pending)], recv_sem=recv_sem.at[receive],
            device_id=device, device_id_type=MESH,
        )
        copy.start()
        pending.append(copy)

    def arrived(dst, receive):
        pltpu.make_async_remote_copy(
            src_ref=dst, dst_ref=dst, send_sem=send_sem.at[0], recv_sem=recv_sem.at[receive],
            device_id={"ch": sibling}, device_id_type=MESH,
        ).wait_recv()

    embed[...] = jnp.zeros_like(embed)
    loads = {}
    for name, src, dst in (
        ("tokens", tokens_in, tokens_ref),
        ("embedding", embedding_in, embedding_ref),
        ("hidden", hidden_in, hidden_ref),
        ("cot", cot_in.at[pl.ds(0, half)], cot_near),
        ("order", order_in, order_ref),
        ("w_in", w_in_in, w_in_ref),
        ("w_gate", w_gate_in, w_gate_ref),
        ("w_out", w_out_in, w_out_ref),
        ("conv_w", conv_w_in, conv_w_ref),
        ("gain", gain_in, gain_ref),
    ):
        loads[name] = pltpu.make_async_copy(src, dst, local_sem.at[len(loads)])
        loads[name].start()
    stores = []

    def store_out(src, dst):
        copy = pltpu.make_async_copy(src, dst, local_sem.at[len(loads) + len(stores)])
        copy.start()
        stores.append(copy)

    for name in ("tokens", "embedding", "hidden"):
        loads[name].wait()
    embed[0:4, :] = embedding_ref[...]
    hot = (lax.broadcasted_iota(jnp.int32, (16, rows), 0) == tokens_ref[...]).astype(F32).astype(BF16)
    looked_up = dot(hot, embed[...], (0, 0))
    block_in[ch] = (hidden_ref[...].astype(F32) + looked_up).astype(BF16)

    pl.semaphore_wait(barrier, len(greeted))

    parts = ((rows - FWD_LEFT, FWD_LEFT), (0, FWD_RIGHT), (FWD_RIGHT, rows - FWD_LEFT - FWD_RIGHT))
    gather = base("gather", 3 * groups)

    def gather_part(i, slot):
        return block_in.at[slot, pl.ds(parts[i][0], parts[i][1])]

    def gather_send(i, slot, target):
        send(gather_part(i, slot), gather_part(i, slot), gather + i * groups + slot, {"ch": target})

    def gather_wait(i, slot):
        arrived(gather_part(i, slot), gather + i * groups + slot)

    for i in range(3):
        gather_send(i, ch, across)
    send(block_in.at[ch], block_in.at[ch], gather + ch, {"ch": sibling})
    cot_sem = base("cot", 1)
    send(cot_in.at[pl.ds(half, half)], cot_far, cot_sem, {"seq": mirror})

    loads["order"].wait()
    for start in range(0, full, 128):
        place = lax.broadcasted_iota(jnp.int32, (128, full), 0) + start
        permute[start : start + 128, :] = (place == order_ref[...]).astype(F32).astype(BF16)
    flip = (
        lax.broadcasted_iota(jnp.int32, (2 * eighth, 2 * eighth), 0)
        + lax.broadcasted_iota(jnp.int32, (2 * eighth, 2 * eighth), 1)
        == 2 * eighth - 1
    ).astype(F32).astype(BF16)

    def terms(source, part):
        value = dot(source[...], w_out_ref[...], (1, 1)).astype(BF16)
        for q in range(groups):
            start = q * eighth if part == 0 else half - eighth - q * eighth
            span = slice(part * eighth, (part + 1) * eighth)
            term_send[q, span, :] = value[start : start + eighth]
            cot_mix[q, span, :] = source[start : start + eighth, :]

    loads["cot"].wait()
    loads["w_out"].wait()
    terms(cot_near, 0)

    def project(i, weights):
        start, size = parts[i]
        total = jnp.zeros((size, width), F32)
        for k in range(groups):
            total = total + dot(block_in[k, start : start + size, :], weights[k * width : (k + 1) * width, :], (1, 0))
        return total

    loads["w_in"].wait()
    halo = base("halo", 2)
    for i in range(2):
        gather_wait(i, across)
        gather_send(i, across, sibling)
    for i in range(2):
        start, size = parts[i]
        if i == 0:
            arrived(block_in.at[sibling], gather + sibling)
        gather_wait(i, diagonal)
        projected = project(i, w_in_ref).astype(BF16)
        level0[FWD_LEFT + start : FWD_LEFT + start + size, :] = projected.astype(F32)
        keep = pl.ds(0, FWD_LEFT) if i == 0 else pl.ds(FWD_LEFT, FWD_RIGHT)
        halo_send[keep, :] = projected
        send(halo_send.at[keep], halo_recv.at[keep], halo + i, {"seq": after if i == 0 else before})
    gather_wait(2, across)
    gather_send(2, across, sibling)
    loads["w_gate"].wait()
    for i in range(2):
        start, size = parts[i]
        gate_pre[start : start + size, :] = project(i, w_gate_ref)

    arrived(cot_far, cot_sem)
    terms(cot_far, 1)
    term = base("term", 3)
    gather_wait(2, diagonal)
    for i in range(2):
        target = i * 2 + 1 - core
        send(term_send.at[target], term_recv.at[i], term + i, {"ch": sibling})
    start, size = parts[2]
    level0[FWD_LEFT + start : FWD_LEFT + start + size, :] = project(2, w_in_ref).astype(BF16).astype(F32)
    gate_pre[start : start + size, :] = project(2, w_gate_ref)

    loads["conv_w"].wait()
    loads["gain"].wait()
    arrived(halo_recv.at[pl.ds(0, FWD_LEFT)], halo)
    arrived(halo_recv.at[pl.ds(FWD_LEFT, FWD_RIGHT)], halo + 1)
    own = FWD_LEFT + rows
    level0[0:FWD_LEFT, :] = halo_recv[0:FWD_LEFT, :].astype(F32) * left_live
    level0[own : own + FWD_RIGHT, :] = halo_recv[FWD_LEFT : FWD_LEFT + FWD_RIGHT, :].astype(F32) * right_live

    def convolve(source, level, sign, lo, hi, live, store):
        dilation = DILATIONS[level]
        for start, size in pieces(lo, hi):
            total = jnp.zeros((size, width), F32)
            for t in range(4):
                begin = start + sign * (t - 2) * dilation
                total = total + conv_w_ref[level, t : t + 1, :] * source[begin : begin + size, :]
            if live is not None:
                total = total * live
            store(start, size, total.astype(BF16).astype(F32))

    def into(target):
        def store(start, size, value):
            target[start : start + size, :] = value
        return store

    for level, (source, target) in enumerate(((level0, level1), (level1, level2))):
        lo, hi = ((8, own + 72), (24, own + 64))[level]
        convolve(source, level, 1, lo, FWD_LEFT, left_live, into(target))
        convolve(source, level, 1, FWD_LEFT, own, None, into(target))
        convolve(source, level, 1, own, hi, right_live, into(target))

    def store_gated(start, size, value):
        start = start - FWD_LEFT
        level3[start : start + size, :] = value
        gate = gate_pre[start : start + size, :]
        gated[start : start + size, :] = (value * (gate * jax.nn.sigmoid(gate))).astype(BF16)

    convolve(level2, 2, 1, FWD_LEFT, own, None, store_gated)

    mix = base("mix", 2 * groups)
    for q in range(groups):
        send(
            gated.at[pl.ds(rows - eighth - q * eighth, eighth)], both.at[ch, pl.ds(eighth, eighth)],
            mix + groups + ch, {"seq": mirror, "ch": q},
        )
    for d in range(1, groups):
        q = lax.rem(ch + d, groups)
        send(gated.at[top(q)], both.at[ch, pl.ds(0, eighth)], mix + ch, {"ch": q})
    both[ch, 0:eighth, :] = gated[top(ch), :]

    for i in range(2):
        arrived(term_recv.at[i], term + i)
    term_send[across] = (term_send[across].astype(F32) + term_recv[1 - x_lo].astype(F32)).astype(BF16)
    send(term_send.at[across], term_cross, term + 2, {"ch": across})
    arrived(term_cross, term + 2)
    grad_norm = term_send[ch].astype(F32) + term_recv[x_lo].astype(F32) + term_cross[...].astype(F32)
    scaled = grad_norm * gain_ref[...]

    for d in range(1, groups):
        q = lax.rem(ch + d, groups)
        arrived(both.at[q, pl.ds(0, eighth)], mix + q)
    for q in range(groups):
        arrived(both.at[q, pl.ds(eighth, eighth)], mix + groups + q)

    mine = jnp.concatenate([both[q] for q in range(groups)], axis=1)
    other = dot(flip, dot(mine, permute[...], (1, 0)).astype(BF16), (1, 0))
    combined = mine.astype(F32) + other
    inv_scale = lax.rsqrt(jnp.mean(combined * combined, axis=1, keepdims=True) + EPSILON)
    hat = combined * inv_scale
    normalized = (hat * gain_ref[...]).astype(BF16)
    norm_mix[ch] = normalized
    row_total = jnp.sum(scaled * hat, axis=1, keepdims=True)
    grad_comb = (inv_scale * (scaled - hat * (row_total * (1.0 / full)))).astype(BF16)
    turned = dot(flip, dot(grad_comb, permute[...], (1, 1)).astype(BF16), (1, 0))
    returned = (grad_comb.astype(F32) + turned).astype(BF16)
    for q in range(groups):
        grad_split[q] = returned[:, q * width : (q + 1) * width]
    back = base("back", 2 * groups)
    for q in range(groups):
        send(
            grad_split.at[q, pl.ds(eighth, eighth)], grad_gated.at[bottom(ch)],
            back + groups + ch, {"seq": mirror, "ch": q},
        )
    for d in range(1, groups):
        q = lax.rem(ch + d, groups)
        send(grad_split.at[q, pl.ds(0, eighth)], grad_gated.at[top(ch)], back + ch, {"ch": q})
    grad_gated[top(ch), :] = grad_split[ch, 0:eighth, :]

    norm = base("norm", groups)

    def norm_send(q, target):
        send(norm_mix.at[q], norm_mix.at[q], norm + q, {"ch": target})

    def norm_wait(q):
        arrived(norm_mix.at[q], norm + q)

    norm_send(ch, across)
    norm_send(ch, sibling)

    conv_rows = 16
    size = full // ring
    part = size // ring
    lanes = width // 2
    of_out, of_gate, late = 0, 1, 2
    finished = (grad_out_ref, grad_gate_ref, grad_in_ref)
    results = (grad_out_out, grad_gate_out, grad_in_out)

    def side(h):
        return slice(lanes * h, lanes * h + lanes)

    def span1(u):
        return pl.ds(0, size + (conv_rows if u == late else 0))

    def sem1(u, h, k):
        return base(("sum", u), 2 * ring) + h * ring + k

    def spread(u, value):
        for h in range(2):
            for k in range(ring):
                send1[u, h, k, 0:size, :] = value[k * size : (k + 1) * size, side(h)].astype(BF16)
        for d in range(1, ring):
            for h in range(2):
                t = lax.rem(me1[h] + d, ring)
                send(
                    send1.at[u, h, t, span1(u)], recv1.at[u, h, me1[h], span1(u)], sem1(u, h, me1[h]),
                    first_peer(h, t),
                )

    def span2(u):
        return pl.ds(u * part, part + (conv_rows if u == late else 0))

    def sem2(u, h, k):
        return base(("over", u), 2 * ring) + h * ring + k

    def second_sum(u):
        for h in range(2):
            total = send1[u, h, me1[h], 0:size, :].astype(F32)
            for d in range(1, ring):
                k = lax.rem(me1[h] + d, ring)
                arrived(recv1.at[u, h, k, span1(u)], sem1(u, h, k))
                total = total + recv1[u, h, k, 0:size, :].astype(F32)
            total = total.astype(BF16)
            for k in range(ring):
                send2[h, k, u * part : (u + 1) * part, :] = total[k * part : (k + 1) * part]
            if u == late:
                recv1[u, h, me1[h], size:, :] = send1[u, h, me1[h], size:, :]
                tail = jnp.zeros((conv_rows, lanes), F32)
                for k in range(ring):
                    tail = tail + recv1[u, h, k, size:, :].astype(F32)
                for k in range(ring):
                    send2[h, k, 3 * part :, :] = tail.astype(BF16)
            span = span2(u)
            for d in range(1, ring):
                t = lax.rem(me2[h] + d, ring)
                send(send2.at[h, t, span], recv2.at[h, me2[h], span], sem2(u, h, me2[h]), second_peer(h, my_x, t))
            recv2[h, me2[h], span, :] = send2[h, me2[h], span, :]

    def sem_x(u, h, x):
        return base(("cross", u), 2 * xs) + h * xs + x

    def cross(u):
        span = span2(u)
        for h in range(2):
            for d in range(1, ring):
                k = lax.rem(me2[h] + d, ring)
                arrived(recv2.at[h, k, span], sem2(u, h, k))
            total = recv2[h, 0, span, :].astype(F32)
            for k in range(1, ring):
                total = total + recv2[h, k, span, :].astype(F32)
            here = cross_x.at[h, my_x, span]
            here[...] = total.astype(BF16)
            for dx in range(1, xs):
                send(here, here, sem_x(u, h, my_x), at(lax.rem(my_x + dx, xs), my_z, my_y))

    def sem3(u, h, k):
        return base(("gather2", u), 2 * ring) + h * ring + k

    def sem4(u, h, k):
        return base(("gather1", u), 2 * ring) + h * ring + k

    def rows_of(k, m=None):
        if m is None:
            return pl.ds(pl.multiple_of(k * size, size), size)
        return pl.ds(pl.multiple_of(k * size + m * part, part), part)

    def done(u, h, k, m=None):
        return finished[u].at[rows_of(k, m), pl.ds(lanes * h, lanes)]

    def second_gather(u):
        span = span2(u)
        for h in range(2):
            for dx in range(1, xs):
                x = lax.rem(my_x + dx, xs)
                arrived(cross_x.at[h, x, span], sem_x(u, h, x))
            total = cross_x[h, 0, span, :].astype(F32)
            for x in range(1, xs):
                total = total + cross_x[h, x, span, :].astype(F32)
            here = done(u, h, me1[h], me2[h])
            here[...] = total[0:part].astype(BF16)
            for d in range(1, ring):
                send(here, here, sem3(u, h, me2[h]), second_peer(h, my_x, lax.rem(me2[h] + d, ring)))
            if u == late:
                for level in range(3):
                    low = part + 4 * level
                    grad_conv_ref[level, :, side(h)] = total[low : low + 4]

    def first_gather(u):
        for h in range(2):
            for d in range(1, ring):
                k = lax.rem(me2[h] + d, ring)
                arrived(done(u, h, me1[h], k), sem3(u, h, k))
            here = done(u, h, me1[h])
            for d in range(1, ring):
                if u == late or d != ring // 2:
                    send(here, here, sem4(u, h, me1[h]), first_peer(h, lax.rem(me1[h] + d, ring)))

    def relay(u):
        for h in range(2):
            k = lax.rem(me1[h] + ring // 2 - 1, ring)
            here = done(u, h, k)
            if ring > 2:
                arrived(here, sem4(u, h, k))
            send(here, here, sem4(u, h, k), first_peer(h, lax.rem(me1[h] + ring - 1, ring)))

    def finish(u):
        for h in range(2):
            for d in range(1, ring):
                k = lax.rem(me1[h] + d, ring)
                if u == late or ring == 2 or d != ring // 2 - 1:
                    arrived(done(u, h, k), sem4(u, h, k))
                if u == late and h == 1:
                    store_out(finished[u].at[rows_of(k)], results[u].at[rows_of(k)])
        if u == late:
            store_out(finished[u].at[rows_of(me1[1])], results[u].at[rows_of(me1[1])])
        else:
            store_out(finished[u], results[u])

    for d in range(1, groups):
        q = lax.rem(ch + d, groups)
        arrived(grad_gated.at[top(q)], back + q)
    for q in range(groups):
        arrived(grad_gated.at[bottom(q)], back + groups + q)
    own = BWD_LEFT + rows
    for start, tall in pieces(0, rows):
        gate = gate_pre[start : start + tall, :]
        sigmoid = jax.nn.sigmoid(gate)
        grad = grad_gated[start : start + tall, :].astype(F32)
        upstream = (grad * (gate * sigmoid)).astype(BF16)
        up3_low[start : start + tall, :] = upstream
        up3[BWD_LEFT + start : BWD_LEFT + start + tall, :] = upstream.astype(F32)
        gate_low[start : start + tall, :] = (
            grad * level3[start : start + tall, :] * sigmoid * (1.0 + gate * (1.0 - sigmoid))
        ).astype(BF16)
    halo_back = base("halo_back", 2)
    send(up3_low.at[pl.ds(0, BWD_RIGHT)], halo_late.at[pl.ds(BWD_LEFT, BWD_RIGHT)], halo_back, {"seq": before})
    send(
        up3_low.at[pl.ds(rows - BWD_LEFT, BWD_LEFT)], halo_late.at[pl.ds(0, BWD_LEFT)], halo_back + 1, {"seq": after}
    )

    def against_input(value):
        return jnp.concatenate([dot(block_in[k], value, (0, 0)) for k in range(groups)], axis=0)

    norm_wait(across)
    norm_send(across, sibling)
    spread(of_gate, against_input(gate_low[...]))
    norm_wait(sibling)
    norm_wait(diagonal)
    spread(of_out, dot(norm_mix[...].reshape(rows, full), cot_mix[...].reshape(rows, width), (0, 0)))

    arrived(halo_late.at[pl.ds(BWD_LEFT, BWD_RIGHT)], halo_back)
    arrived(halo_late.at[pl.ds(0, BWD_LEFT)], halo_back + 1)
    up3[0:BWD_LEFT, :] = halo_late[0:BWD_LEFT, :].astype(F32) * left_live
    up3[own : own + BWD_RIGHT, :] = halo_late[BWD_LEFT : BWD_LEFT + BWD_RIGHT, :].astype(F32) * right_live

    convolve(up3, 2, -1, 64, BWD_LEFT, left_live, into(up2))
    convolve(up3, 2, -1, BWD_LEFT, own, None, into(up2))
    convolve(up3, 2, -1, own, own + 24, right_live, into(up2))
    convolve(up2, 1, -1, 72, BWD_LEFT, left_live, into(up1))
    convolve(up2, 1, -1, BWD_LEFT, own, None, into(up1))
    convolve(up2, 1, -1, own, own + 8, right_live, into(up1))

    def store_last(start, tall, value):
        up0_low[start - BWD_LEFT : start - BWD_LEFT + tall, :] = value.astype(BF16)

    convolve(up1, 0, -1, BWD_LEFT, own, None, store_last)

    taps = []
    for level, (source, upstream) in enumerate(((level0, up1), (level1, up2), (level2, up3))):
        for t in range(4):
            total = jnp.zeros((8, width), F32)
            for start, tall in pieces(0, rows):
                begin = FWD_LEFT + start + (t - 2) * DILATIONS[level]
                term_product = (
                    upstream[BWD_LEFT + start : BWD_LEFT + start + tall, :] * source[begin : begin + tall, :]
                )
                total = total + jnp.sum(term_product.reshape(tall // 8, 8, width), axis=0)
            taps.append(jnp.sum(total, axis=0, keepdims=True))
    taps = jnp.concatenate(taps + [jnp.zeros((conv_rows - 12, width), F32)], axis=0).astype(BF16)
    for h in range(2):
        for k in range(ring):
            send1[late, h, k, size : size + conv_rows, :] = taps[:, side(h)]
    spread(late, against_input(up0_low[...]))

    second_sum(of_gate)

    product = dot(norm_mix[...].reshape(rows, full), w_out_ref[...], (1, 0))
    for q in range(groups):
        near = product[q * 2 * eighth : q * 2 * eighth + eighth]
        low = q * eighth
        output_ref[low : low + eighth, :] = (block_in[ch, low : low + eighth, :].astype(F32) + near).astype(BF16)
        low = half - eighth - q * eighth
        product_send[low : low + eighth, :] = product[q * 2 * eighth + eighth : (q + 1) * 2 * eighth].astype(BF16)
    product_sem = base("product", 1)
    send(product_send, product_recv, product_sem, {"seq": mirror})
    store_out(output_ref.at[pl.ds(0, half)], output_out.at[pl.ds(0, half)])

    second_sum(of_out)
    cross(of_gate)
    second_sum(late)
    second_gather(of_gate)
    cross(of_out)
    arrived(product_recv, product_sem)
    output_ref[half:rows, :] = (
        block_in[ch, half:rows, :].astype(F32) + product_recv[...].astype(F32)
    ).astype(BF16)
    store_out(output_ref.at[pl.ds(half, half)], output_out.at[pl.ds(half, half)])
    cross(late)
    second_gather(of_out)
    first_gather(of_gate)
    second_gather(late)
    first_gather(of_out)
    first_gather(late)
    relay(of_gate)
    relay(of_out)
    store_out(grad_conv_ref, grad_conv_out)
    finish(of_gate)
    finish(of_out)
    for copy in pending:
        copy.wait_send()
    finish(late)
    for copy in stores:
        copy.wait()


def hand_over(*refs):
    count = len(refs) // 3
    given, results, stages, sems = refs[:count], refs[count : 2 * count], refs[2 * count : 3 * count], refs[-1]
    loads = [pltpu.make_async_copy(given[i], stages[i], sems.at[0, i]) for i in range(count)]
    stores = [pltpu.make_async_copy(stages[i], results[i], sems.at[1, i]) for i in range(count)]
    for copy in loads:
        copy.start()
    for load, store in zip(loads, stores):
        load.wait()
        store.start()
    for copy in stores:
        copy.wait()


def local(tokens, hidden, embedding, w_in, w_gate, conv_w, channel_order, gain, w_out, cotangent):
    rows, width = hidden.shape
    full = gain.shape[0]
    groups = lax.axis_size("ch")
    sizes = ring_sizes(lax.axis_size("seq"))
    xs, zs, ys = sizes
    size = full // ys
    part = size // zs
    eighth = rows // (2 * groups)
    extended = rows + FWD_LEFT + FWD_RIGHT
    anywhere = pl.BlockSpec(memory_space=pl.ANY)
    dma = pltpu.SemaphoreType.DMA

    def held(*shape, dtype=BF16):
        return pltpu.VMEM(shape, dtype)

    weight = jax.ShapeDtypeStruct((full, width), BF16)
    results = (
        jax.ShapeDtypeStruct((rows, width), BF16), weight, weight, weight, jax.ShapeDtypeStruct((3, 4, width), F32)
    )
    computed = pl.pallas_call(
        functools.partial(block_kernel, sizes, groups),
        out_shape=results,
        in_specs=[anywhere] * 10,
        out_specs=(anywhere,) * 5,
        scratch_shapes=[
            held(1, rows, dtype=jnp.int32),
            held(rows, width),
            held(4, width),
            held(full, width),
            held(full, width),
            held(3, 4, width, dtype=F32),
            held(1, full, dtype=jnp.int32),
            held(1, full, dtype=F32),
            held(full, width),
            held(rows, width),
            held(full, width),
            held(full, width),
            held(full, width),
            held(3, 4, width, dtype=F32),
            held(groups, rows, width),
            held(16, width),
            held(extended, width, dtype=F32),
            held(extended, width, dtype=F32),
            held(extended, width, dtype=F32),
            held(rows, width, dtype=F32),
            held(rows, width, dtype=F32),
            held(FWD_LEFT + FWD_RIGHT, width),
            held(FWD_LEFT + FWD_RIGHT, width),
            held(BWD_LEFT + BWD_RIGHT, width),
            held(rows, width),
            held(groups, 2 * eighth, width),
            held(full, full),
            held(rows // 2, width),
            held(rows // 2, width),
            held(groups, 2 * eighth, width),
            held(groups, 2 * eighth, full),
            held(2, 2 * eighth, full),
            held(2 * eighth, full),
            held(groups, 2 * eighth, full),
            held(groups, 2 * eighth, width),
            held(rows, width),
            held(extended, width, dtype=F32),
            held(extended, width, dtype=F32),
            held(extended, width, dtype=F32),
            held(rows // 2, width),
            held(rows // 2, width),
            held(rows, width),
            held(rows, width),
            held(rows, width),
            held(3, 2, ys, size + 16, width // 2),
            held(3, 2, ys, size + 16, width // 2),
            held(2, zs, 3 * part + 16, width // 2),
            held(2, zs, 3 * part + 16, width // 2),
            held(2, xs, 3 * part + 16, width // 2),
            dma((SENDS,)),
            dma((RECEIVES,)),
            dma((32,)),
        ],
        compiler_params=pltpu.CompilerParams(
            collective_id=0, has_side_effects=True, vmem_limit_bytes=56 * 1024 * 1024
        ),
    )(
        tokens.reshape(1, rows), hidden, embedding, w_in, w_gate, conv_w, channel_order.reshape(1, full),
        gain.reshape(1, full), w_out, cotangent,
    )
    return pl.pallas_call(
        hand_over,
        out_shape=results,
        in_specs=[anywhere] * 5,
        out_specs=(anywhere,) * 5,
        scratch_shapes=[held(*result.shape, dtype=result.dtype) for result in results] + [dma((2, 5))],
        compiler_params=pltpu.CompilerParams(vmem_limit_bytes=60 * 1024 * 1024),
    )(*computed)


def solution(mesh):
    placed = (
        P("seq"),
        P("seq", "ch"),
        P(None, "ch"),
        P(None, "ch"),
        P(None, "ch"),
        P(None, None, "ch"),
        P(),
        P(),
        P(None, "ch"),
        P("seq", "ch"),
    )
    return jax.shard_map(
        local,
        mesh=mesh,
        in_specs=placed,
        out_specs=(
            P("seq", "ch"),
            P(None, "ch"),
            P(None, "ch"),
            P(None, "ch"),
            P(None, None, "ch"),
        ),
        check_vma=False,
    )
```
